512 devices in a mesh: ctx: 32 (over z, y_lo), head: 16 (over x, y_hi, core).
Axes of the slice: x: 4, y: 8 (y_hi: 2, y_lo: 4; y = y_hi * 4 + y_lo), z: 8, core: 2. Of those that a mesh axis runs over, the one named last changes fastest.
Arguments:
- ssm_input: bfloat16 [4096, 16384], P('ctx', 'head'), may hold values from -6 to 6
- ssm_gate: bfloat16 [4096, 16384], P('ctx', 'head'), may hold values from -60 to 60
- step_size: float32 [4096, 256], P('ctx', 'head'), may hold values from 0.02 to 0.2
- log_decay: float32 [4096, 256], P('ctx', 'head'), may hold values from -2 to 0
- input_b: bfloat16 [4096, 2048], P('ctx', 'head'), may hold values from -1.796875 to 1.796875
- input_c: bfloat16 [4096, 2048], P('ctx', 'head'), may hold values from -1.796875 to 1.796875
- skip_gain: float32 [256], P('head'), may hold values from 0.5 to 1.5
- norm_gain: float32 [16384], P('head'), may hold values from 0.5 to 1.5
- attn_queries: bfloat16 [4096, 8192], P('ctx', 'head'), may hold values from -30 to 30
- attn_keys: bfloat16 [4096, 1024], P('ctx', 'head'), may hold values from -11 to 11
- attn_values: bfloat16 [4096, 1024], P('ctx', 'head'), may hold values from -6 to 6
Outputs:
- ssm_out: bfloat16 [4096, 16384], P('ctx', 'head')
- attn_out: bfloat16 [4096, 8192], P('ctx', 'head')
The draws below stay inside these ranges and needn't reach their ends.
All inputs are finite; a program needn't handle non-finite values.
Results may differ from the reference program's by a relative error of at most 0.01.
Values may be sent and summed in bfloat16 or wider, within the bound.
A program may use at most 128 MiB of HBM per device.

```python
import math
import jax
import jax.numpy as jnp
from jax import lax

P_SIZE = 64
N = 256
HD = 128
SPAN = 128
SEQUENCE_TOKENS = 4096
STATE_HEADS = 256
GROUPS = 8
INNER = 16384
GROUP_W = 2048
QHEADS = 64
KVHEADS = 8


def shared_attention(key):
    base_key = jax.random.fold_in(key, 101)
    sub_keys = jax.random.split(base_key, 1)
    key_width = KVHEADS * HD
    normal_keys = jnp.clip(jax.random.normal(sub_keys[0], (SEQUENCE_TOKENS, key_width), jnp.float32), -6.0, 6.0) * 1.73
    return normal_keys


def draw_attn_keys(key, part):
    normal_keys = shared_attention(key)
    return normal_keys.astype(jnp.bfloat16)


def draw_attn_queries(key, part):
    key = jax.random.fold_in(key, 3)
    query_width = QHEADS * HD
    drawn = jnp.clip(jax.random.normal(key, (SEQUENCE_TOKENS, query_width), jnp.float32), -6.0, 6.0) * 1.73
    return drawn.astype(jnp.bfloat16)


def draw_ssm_gate(key, part):
    key = jax.random.fold_in(key, 5)
    sub_keys = jax.random.split(key, 3)
    columns = (jnp.arange(INNER) % GROUP_W).astype(jnp.float32)
    column_scale = 0.3 * 10.0 ** (columns / (GROUP_W - 1))
    row_scale = 10.0 ** jax.random.uniform(sub_keys[0], (SEQUENCE_TOKENS, 1), jnp.float32, -0.3, 0.7)
    noise = jnp.clip(jax.random.normal(sub_keys[2], (SEQUENCE_TOKENS, INNER), jnp.float32), -4.0, 4.0)
    drawn = noise * row_scale * column_scale[None, :]
    return drawn.astype(jnp.bfloat16)


def draw_log_decay(key, part):
    key = jax.random.fold_in(key, 7)
    sub_keys = jax.random.split(key, 6)
    fast_share = 0.5
    is_fast = jax.random.bernoulli(sub_keys[0], fast_share, (STATE_HEADS,))
    fast_rate = 10.0 ** jax.random.uniform(sub_keys[1], (STATE_HEADS,), jnp.float32, math.log10(1.0 / 50.0), math.log10(1.0 / 30.0))
    slow_rate = 10.0 ** jax.random.uniform(sub_keys[2], (STATE_HEADS,), jnp.float32, math.log10(0.05), math.log10(0.3)) / SEQUENCE_TOKENS
    head_decay_rate = jnp.where(is_fast, fast_rate, slow_rate)
    coarse_estimate = jax.random.uniform(sub_keys[3], (SEQUENCE_TOKENS, STATE_HEADS), jnp.float32, 0.5, 1.5)
    marked_positions = jax.random.randint(sub_keys[4], (3,), 0, SEQUENCE_TOKENS)
    loss_values = jax.random.uniform(sub_keys[5], (3, STATE_HEADS), jnp.float32, math.log(0.6), math.log(0.8))
    row_index = jnp.arange(SEQUENCE_TOKENS)[:, None]
    spike_events = jnp.zeros((SEQUENCE_TOKENS, STATE_HEADS), jnp.float32)
    for item_count in range(3):
        spike_events = spike_events + jnp.where(row_index == marked_positions[item_count], loss_values[item_count][None, :], 0.0)
    return -head_decay_rate[None, :] * coarse_estimate + spike_events


def block_scale(own_key, dims, cuts, low, largest):
    def one(dim, parts):
        heights = jax.random.uniform(jax.random.fold_in(jax.random.fold_in(own_key, 6), dim), (parts,), jnp.float32, low / len(cuts), largest / len(cuts))
        return jnp.repeat(jnp.exp(heights), dims[dim] // parts).reshape((-1,) + (1,) * (len(dims) - dim - 1))

    factor_of = one(*cuts[0])
    for cut in cuts[1:]:
        factor_of = factor_of * one(*cut)
    return factor_of


def scatter_about(rng, shape, width, most, cuts=(), kind=jnp.bfloat16):
    factor_of = block_scale(rng, shape, cuts, -0.22, 0.18) if cuts else 1.0
    values = jax.random.normal(rng, shape, jnp.float32) * width * factor_of
    return jnp.minimum(jnp.maximum(values, -most), most).astype(kind)


def setup_inputs(seed: int = 0) -> dict:
    splits = jax.random.split(jax.random.key(seed), 12)
    return {
        "ssm_input": scatter_about(splits[0], (SEQUENCE_TOKENS, INNER), 1.0, 6.0, ((0, 32), (1, 16))),
        "ssm_gate": draw_ssm_gate(jax.random.fold_in(splits[11], 71), 0),
        "step_size": jnp.clip(jnp.exp(math.log(0.2) - 2.3025851 * jax.random.uniform(splits[2], (SEQUENCE_TOKENS, STATE_HEADS), jnp.float32) ** block_scale(splits[2], (SEQUENCE_TOKENS, STATE_HEADS), ((0, 32), (1, 16)), -0.2, 0.2)), 0.02, 0.2),
        "log_decay": draw_log_decay(jax.random.fold_in(splits[11], 71), 0),
        "input_b": scatter_about(splits[4], (SEQUENCE_TOKENS, GROUPS * N), 0.3, 1.796875, ((0, 32), (1, 16))),
        "input_c": scatter_about(splits[5], (SEQUENCE_TOKENS, GROUPS * N), 0.3, 1.796875, ((0, 32), (1, 16))),
        "skip_gain": jnp.clip(0.5 + 1.0 * jax.random.uniform(splits[6], (STATE_HEADS,), jnp.float32) ** block_scale(splits[6], (STATE_HEADS,), ((0, 16),), -0.2, 0.2), 0.5, 1.5),
        "norm_gain": jnp.clip(1.0 + 0.1 * jax.random.normal(splits[7], (INNER,), jnp.float32), 0.5, 1.5),
        "attn_queries": draw_attn_queries(jax.random.fold_in(splits[11], 71), 0),
        "attn_keys": draw_attn_keys(jax.random.fold_in(splits[11], 71), 0),
        "attn_values": scatter_about(splits[10], (SEQUENCE_TOKENS, KVHEADS * HD), 1.0, 6.0, ((0, 32), (1, 16))),
    }


EPSILON = 1e-05

def ssd_layer(ssm_input, ssm_gate, step_size, log_decay, input_b, input_c, skip_gain, norm_gain):
    total_rows = ssm_input.shape[0]
    head_count = step_size.shape[1]
    group_count = input_b.shape[1] // N
    per_group = head_count // group_count
    block_count = total_rows // SPAN
    inputs_x = ssm_input.reshape(block_count, SPAN, head_count, P_SIZE)
    steps_dt = step_size.reshape(block_count, SPAN, head_count)
    decays = log_decay.reshape(block_count, SPAN, head_count)
    blocks_b = input_b.reshape(block_count, SPAN, group_count, N)
    blocks_c = input_c.reshape(block_count, SPAN, group_count, N)
    lower_tri = jnp.arange(SPAN)[:, None] >= jnp.arange(SPAN)[None, :]

    def one_block(carried, pieces):
        block_x, block_dt, block_decay, block_b, block_c = pieces
        cum_decay = jnp.cumsum(block_decay, axis=0)
        wide_x = block_x.astype(jnp.float32)
        wide_b = block_b.astype(jnp.float32)
        wide_c = block_c.astype(jnp.float32)
        inner_cb = jnp.repeat(jnp.einsum('qgn,kgn->gqk', wide_c, wide_b), per_group, axis=0)
        cum_heads = cum_decay.T
        decay_gaps = cum_heads[:, :, None] - cum_heads[:, None, :]
        decay_mat = jnp.where(lower_tri, jnp.exp(jnp.where(lower_tri, decay_gaps, 0.0)), 0.0)
        mix_matrix = (inner_cb * decay_mat * block_dt.T[:, None, :]).astype(jnp.bfloat16)
        within = jnp.einsum('hqk,khp->qhp', mix_matrix.astype(jnp.float32), wide_x)
        head_b = jnp.repeat(wide_b, per_group, axis=1)
        head_c = jnp.repeat(wide_c, per_group, axis=1)
        from_state = jnp.exp(cum_decay)[:, :, None] * jnp.einsum('qhn,hnp->qhp', head_c, carried, precision=lax.Precision.HIGHEST)
        weight = jnp.exp(cum_decay[-1][None, :] - cum_decay) * block_dt
        new_state = jnp.exp(cum_decay[-1])[:, None, None] * carried + jnp.einsum('khn,khp->hnp', head_b, wide_x * weight[:, :, None], precision=lax.Precision.HIGHEST)
        output = within + from_state + skip_gain[None, :, None] * wide_x
        return (new_state, output)
    start_state = jnp.zeros((head_count, N, P_SIZE), jnp.float32)
    final_state, outputs = lax.scan(one_block, start_state, (inputs_x, steps_dt, decays, blocks_b, blocks_c))
    ssm_y = outputs.reshape(total_rows, head_count * P_SIZE)
    gated = ssm_y * jax.nn.silu(ssm_gate.astype(jnp.float32))
    grouped = gated.reshape(total_rows, group_count, -1)
    mean_sq = lax.optimization_barrier(jnp.mean(grouped * grouped, axis=-1, keepdims=True))
    normed = (grouped * lax.rsqrt(mean_sq + EPSILON)).reshape(total_rows, head_count * P_SIZE)
    return (normed * norm_gain[None, :]).astype(jnp.bfloat16)

def attention_layer(attn_queries, attn_keys, attn_values):
    total_rows = attn_queries.shape[0]
    query_heads = attn_queries.shape[1] // HD
    key_heads = attn_keys.shape[1] // HD
    per_key = query_heads // key_heads
    block_rows = math.gcd(total_rows, 1024)
    score_scale = 1.0 / math.sqrt(HD)
    positions = jnp.arange(total_rows, dtype=jnp.int32)
    queries = attn_queries.reshape(total_rows, query_heads, HD)
    keys_all = attn_keys.reshape(total_rows, key_heads, HD)
    values_all = attn_values.reshape(total_rows, key_heads, HD)

    def one_head(head_id):
        head_q = lax.dynamic_index_in_dim(queries, head_id, 1, keepdims=False)
        head_k = lax.dynamic_index_in_dim(keys_all, head_id // per_key, 1, keepdims=False)
        head_v = lax.dynamic_index_in_dim(values_all, head_id // per_key, 1, keepdims=False)
        outputs = []
        for item_count in range(total_rows // block_rows):
            first_row = item_count * block_rows
            last_row = first_row + block_rows
            scores = jnp.dot(head_q[first_row:last_row], head_k[:last_row].T, preferred_element_type=jnp.float32) * score_scale
            visible = positions[None, :last_row] <= positions[first_row:last_row, None]
            scores = jnp.where(visible, scores, -jnp.inf)
            row_top = lax.optimization_barrier(jnp.max(scores, axis=-1, keepdims=True))
            raw_weights = jnp.where(visible, jnp.exp(scores - row_top), 0.0)
            denominator = lax.optimization_barrier(jnp.sum(raw_weights, axis=-1, keepdims=True))
            weights = raw_weights.astype(jnp.bfloat16)
            mixed_rows = jnp.dot(weights, head_v[:last_row], preferred_element_type=jnp.float32) / denominator
            outputs.append(mixed_rows.astype(jnp.bfloat16))
        return jnp.concatenate(outputs, axis=0)
    heads_out = lax.map(one_head, jnp.arange(query_heads, dtype=jnp.int32))
    return jnp.transpose(heads_out, (1, 0, 2)).reshape(total_rows, query_heads * HD)

def reference(ssm_input, ssm_gate, step_size, log_decay, input_b, input_c, skip_gain, norm_gain, attn_queries, attn_keys, attn_values):
    ssm_out = ssd_layer(ssm_input, ssm_gate, step_size, log_decay, input_b, input_c, skip_gain, norm_gain)
    attn_out = attention_layer(attn_queries, attn_keys, attn_values)
    return (ssm_out, attn_out)
```

```python
import functools
import math

import jax
import jax.numpy as jnp
from jax import lax
from jax.experimental import pallas as pl
from jax.experimental.pallas import tpu as pltpu
from jax.sharding import PartitionSpec as P

MESH = pl.DeviceIdType.MESH
BF = jnp.bfloat16
F32 = jnp.float32
HI = lax.Precision.HIGHEST

TOK = 128
NZ, NY = 8, 4
HEADS = 16
QW = 256
QH = 4
EPSILON = 1e-05
NEGATIVE = -1e30
SCALE = 1.0 / math.sqrt(128)

NT = (((1,), (1,)), ((), ()))
TN = (((0,), (0,)), ((), ()))


def dot(a, b, dims=(((1,), (0,)), ((), ())), precision=None):
    return lax.dot_general(a, b, dims, precision=precision, preferred_element_type=F32)


def kernel(
    x_hbm, gate_hbm, dt_hbm, ld_hbm, b_hbm, c_hbm, skip_ref, gain_ref, q_hbm, k_hbm, v_hbm,
    ssm_out, attn_out,
    x_ref, gate_ref, dt_ref, ld_ref, q_ref, halves, khalf, vhalf,
    brow, crow, xrow, pk, prow, tb, zin, lam_out, lam_in, rz, rin, early, gout, fs,
    kv, m_ref, l_ref, acc_ref, yb, sq_out, sq_in,
    load_sem, pair_s, pair_r, y_s, y_r, z_s, z_r, kvy_s, kvy_r, kvp_s, kvp_r, kvm_s, kvm_r, kvh_s, kvh_r,
):
    ctx = lax.axis_index("ctx")
    head = lax.axis_index("head")
    z, y = lax.div(ctx, NY), lax.rem(ctx, NY)
    core = lax.rem(head, 2)
    partner = (ctx, head + 1 - 2 * core)
    y_peer = [None] + [(z * NY + lax.rem(y + k, NY), head) for k in range(1, NY)]
    z_peer = [None] + [(lax.rem(z + k, NZ) * NY + y, head) for k in range(1, NZ)]
    y_at = [lax.rem(y + k, NY) for k in range(NY)]
    z_at = [lax.rem(z + k, NZ) for k in range(NZ)]

    barrier = pltpu.get_barrier_semaphore()
    for peer in [partner] + y_peer[1:] + z_peer[1:]:
        pl.semaphore_signal(barrier, inc=1, device_id=peer, device_id_type=MESH)

    loads = [
        pltpu.make_async_copy(src, dst, load_sem.at[i])
        for i, (src, dst) in enumerate(
            [
                (dt_hbm, dt_ref),
                (ld_hbm, ld_ref),
                (k_hbm, khalf.at[core]),
                (v_hbm, vhalf.at[core]),
                (b_hbm, brow.at[y, core]),
                (c_hbm, crow.at[y, core]),
                (x_hbm, x_ref),
                (x_hbm.at[:, pl.ds(pl.multiple_of(y * QW, QW), QW)], xrow.at[y]),
                (q_hbm, q_ref),
                (gate_hbm, gate_ref),
            ]
        )
    ]
    for load in loads:
        load.start()

    sends = []

    def send(src, dst, s_sem, r_sem, device):
        copy = pltpu.make_async_remote_copy(
            src_ref=src, dst_ref=dst, send_sem=s_sem, recv_sem=r_sem, device_id=device, device_id_type=MESH
        )
        copy.start()
        sends.append(copy)
        return copy

    loads[0].wait()
    loads[1].wait()
    row = lax.broadcasted_iota(jnp.int32, (TOK, TOK), 0)
    col = lax.broadcasted_iota(jnp.int32, (TOK, TOK), 1)
    lower = col <= row
    tri = lower.astype(F32)
    eye = (row == col).astype(F32)
    lane = lax.broadcasted_iota(jnp.int32, (1, TOK), 1)
    left = lane < 64
    ld = ld_ref[...]
    cum = dot(tri, ld, precision=HI)
    cum_t = dot(ld, (row <= col).astype(F32), TN, precision=HI)
    dt_t = dot(dt_ref[...], eye, TN, precision=HI)
    block_log = cum_t[:, TOK - 1 : TOK]
    weight_t = jnp.exp(block_log - cum_t) * dt_t
    log_t = jnp.broadcast_to(block_log, (HEADS, TOK))
    for quarter in range(NY):
        heads = slice(4 * quarter, 4 * quarter + 4)
        pk[quarter] = jnp.concatenate([weight_t[heads], log_t[heads]], axis=0)
    prow[y] = pk[y]
    for i in (2, 3, 4, 5):
        loads[i].wait()

    pl.semaphore_wait(barrier, 1 + (NY - 1) + (NZ - 1))

    pair_k = send(khalf.at[core], khalf.at[core], pair_s.at[0], pair_r.at[0], partner)
    pair_v = send(vhalf.at[core], vhalf.at[core], pair_s.at[1], pair_r.at[1], partner)
    pair_b = send(brow.at[y, core], brow.at[y, core], pair_s.at[2], pair_r.at[2], partner)
    pair_c = send(crow.at[y, core], crow.at[y, core], pair_s.at[3], pair_r.at[3], partner)
    y_pk, y_b, y_x, y_c = [None], [None], [None], [None]
    for k in range(1, NY):
        y_b.append(send(brow.at[y, core], brow.at[y, core], y_s.at[0, k], y_r.at[0, k], y_peer[k]))
        y_pk.append(send(pk.at[y_at[k]], prow.at[y], y_s.at[1, k], y_r.at[1, k], y_peer[k]))
    for k in range(1, NY):
        quarter = x_hbm.at[:, pl.ds(pl.multiple_of(y_at[k] * QW, QW), QW)]
        y_x.append(send(quarter, xrow.at[y], y_s.at[2, k], y_r.at[2, k], y_peer[k]))

    pair_k.wait_recv()
    pair_v.wait_recv()
    kv[0, 0, 0] = jnp.concatenate([khalf[0], khalf[1]], axis=1)
    kv[1, 0, 0] = jnp.concatenate([vhalf[0], vhalf[1]], axis=1)

    plus, minus, row_kv, hand = {}, {}, {}, {}

    def send_plus(s, k):
        plus[s, k] = send(
            kv.at[core, s, k], kv.at[core, s + 1, k], kvp_s.at[s, k], kvp_r.at[s, k], z_peer[1]
        )

    def send_minus(s, k):
        minus[s, k] = send(
            kv.at[core, (NZ - s) % NZ, k], kv.at[core, 7 - s, k], kvm_s.at[s, k], kvm_r.at[s, k], z_peer[NZ - 1]
        )

    def hand_over(i, slot, first):
        part = kv.at[core, slot, pl.ds(first, NY - first)]
        hand[slot] = send(part, part, kvh_s.at[i], kvh_r.at[i], partner)

    def pump(s, blocks):
        for k in blocks:
            plus[s, k].wait_recv()
            if s < 3:
                send_plus(s + 1, k)
            if s < 3:
                minus[s, k].wait_recv()
                if s < 2:
                    send_minus(s + 1, k)

    def hand_rows(s):
        hand_over(1 + 2 * s, s + 1, 0)
        if s < 3:
            hand_over(2 + 2 * s, 7 - s, 0)

    send_plus(0, 0)
    send_minus(0, 0)
    for k in range(1, NY):
        row_kv[k] = send(kv.at[core, 0, 0], kv.at[core, 0, NY - k], kvy_s.at[k], kvy_r.at[k], y_peer[k])

    loads[8].wait()

    def attend(keys, values, first=False):
        for h in range(QH):
            scores = dot(q_ref[:, h * 128 : (h + 1) * 128], keys, NT)
            if first:
                scores = jnp.where(lower, scores, NEGATIVE)
                top = jnp.max(scores, axis=1, keepdims=True)
                weights = jnp.exp((scores - top) * SCALE)
                total = jnp.sum(weights, axis=1, keepdims=True)
                mixed = dot(weights.astype(BF), values)
            else:
                before = m_ref[h][:, :1]
                top = jnp.maximum(before, jnp.max(scores, axis=1, keepdims=True))
                factor = jnp.exp((before - top) * SCALE)
                weights = jnp.exp((scores - top) * SCALE)
                total = l_ref[h][:, :1] * factor + jnp.sum(weights, axis=1, keepdims=True)
                mixed = acc_ref[h] * factor + dot(weights.astype(BF), values)
            m_ref[h] = jnp.broadcast_to(top, (TOK, 128))
            l_ref[h] = jnp.broadcast_to(total, (TOK, 128))
            acc_ref[h] = mixed

    def attend_row(slot):
        @pl.when(z >= slot)
        def _():
            attend(kv[0, slot].reshape(NY * TOK, 128), kv[1, slot].reshape(NY * TOK, 128))

    attend(kv[0, 0, 0], kv[1, 0, 0], first=True)

    pair_b.wait_recv()
    pair_c.wait_recv()
    loads[6].wait()
    inner = dot(crow[y, 0], brow[y, 0], NT) + dot(crow[y, 1], brow[y, 1], NT)
    for i in range(HEADS // 2):
        cols = slice(128 * i, 128 * (i + 1))
        x_two = x_ref[:, cols]
        parts = []
        for h in (2 * i, 2 * i + 1):
            gap = jnp.where(lower, cum[:, h : h + 1] - cum_t[h : h + 1, :], NEGATIVE)
            mix = (inner * jnp.exp(gap) * dt_t[h : h + 1, :]).astype(BF)
            parts.append(dot(mix, x_two))
        gain = jnp.where(left, skip_ref[:, 2 * i : 2 * i + 1], skip_ref[:, 2 * i + 1 : 2 * i + 2])
        yb[:, cols] = jnp.where(left, parts[0], parts[1]) + gain * x_two.astype(F32)

    pump(0, [0])

    hand_b = [None]
    for k in range(1, NY):
        y_b[k].wait_recv()
        part = brow.at[y_at[NY - k], core]
        hand_b.append(send(part, part, pair_s.at[3 + k], pair_r.at[3 + k], partner))
    pump(1, [0])
    loads[7].wait()
    for k in range(1, NY):
        y_pk[k].wait_recv()
        y_x[k].wait_recv()
    for k in range(1, NY):
        hand_b[k].wait_recv()
    packed = prow[...]
    columns = packed.reshape(NY * 8, TOK).T

    def two_by_two(parts):
        return jnp.concatenate(
            [jnp.where(left, parts[0], parts[1]), jnp.where(left, parts[2], parts[3])], axis=1
        )

    logs = [two_by_two([packed[j, 4 + i : 5 + i] for i in range(4)]) for j in range(NY)]
    lam_out[...] = jnp.broadcast_to(logs[0] + logs[1] + logs[2] + logs[3], (8, QW))
    z_lam = [None]
    for k in range(1, NZ):
        z_lam.append(send(lam_out, lam_in.at[z], z_s.at[0, k], z_r.at[0, k], z_peer[k]))
    lam_in[z] = lam_out[...]
    state = None
    priors = [None]
    for j in range(NY):
        weight = two_by_two([columns[:, 8 * j + i : 8 * j + i + 1] for i in range(4)])
        weighted = (xrow[j].astype(F32) * weight).astype(BF)
        own = jnp.concatenate([dot(brow[j, 0], weighted, TN), dot(brow[j, 1], weighted, TN)], axis=0)
        state = own if state is None else state * jnp.exp(logs[j]) + own
        priors.append(state)
    tb[...] = state.astype(BF).reshape(NZ, 32, QW)
    z_one = [None]
    for k in range(1, NZ):
        z_one.append(send(tb.at[z_at[k]], zin.at[z], z_s.at[1, k], z_r.at[1, k], z_peer[k]))
    zin[z] = tb[z]
    for k in range(1, NY):
        y_c.append(send(crow.at[y, core], crow.at[y, core], y_s.at[3, k], y_r.at[3, k], y_peer[k]))

    pump(2, [0])
    for k in range(1, NY):
        row_kv[k].wait_recv()
        send_plus(0, NY - k)
        send_minus(0, NY - k)
    hand_over(0, 0, 1)
    pump(3, [0])

    hand_c = [None]
    for k in range(1, NY):
        y_c[k].wait_recv()
        part = crow.at[y_at[NY - k], core]
        hand_c.append(send(part, part, pair_s.at[6 + k], pair_r.at[6 + k], partner))
    for k in range(1, NY):
        hand_c[k].wait_recv()
    for j in range(1, NY):
        prior = priors[j].astype(BF)
        early[j] = dot(crow[j, 0], prior[:128]) + dot(crow[j, 1], prior[128:])

    for k in range(1, NZ):
        z_lam[k].wait_recv()
        z_one[k].wait_recv()
    state = jnp.zeros((32, QW), F32)
    for r in range(NZ):
        rz[r] = state.astype(BF)
        if r < NZ - 1:
            state = state * jnp.exp(lam_in[r, 0:1]) + zin[r].astype(F32)
    z_two = [None]
    for k in range(1, NZ):
        z_two.append(send(rz.at[z_at[k]], rin.at[z], z_s.at[2, k], z_r.at[2, k], z_peer[k]))
    rin[z] = rz[z]

    hand[0].wait_recv()
    for k in range(1, NY):

        @pl.when(y + k >= NY)
        def _():
            attend(kv[0, 0, k], kv[1, 0, k])

    pump(0, [1, 2, 3])
    hand_rows(0)
    pump(1, [1, 2, 3])
    hand_rows(1)
    hand[1].wait_recv()
    attend_row(1)

    for k in range(1, NZ):
        z_two[k].wait_recv()
    entering = rin[...].reshape(QW, QW)
    before = jnp.zeros((1, QW), F32)
    for j in range(NY):
        part = dot(crow[j, 0], entering[:128]) + dot(crow[j, 1], entering[128:])
        if j > 0:
            before = before + logs[j - 1]
            part = part * jnp.exp(before) + early[j]
        gout[j] = part.astype(BF)
    y_out = [None]
    for k in range(1, NY):
        y_out.append(send(gout.at[y_at[k]], fs.at[y], y_s.at[4, k], y_r.at[4, k], y_peer[k]))
    fs[y] = gout[y]

    pump(2, [1, 2, 3])
    hand_rows(2)
    hand[7].wait_recv()
    attend_row(7)
    pump(3, [1, 2, 3])
    hand_rows(3)
    for slot in (2, 6, 3, 5, 4):
        hand[slot].wait_recv()
        attend_row(slot)
    for h in range(QH):
        attn_out[:, h * 128 : (h + 1) * 128] = (acc_ref[h] / l_ref[h]).astype(BF)

    for k in range(1, NY):
        y_out[k].wait_recv()
    loads[9].wait()
    decay = jnp.exp(cum)
    squares = jnp.zeros((TOK, 128), F32)
    for i in range(HEADS // 2):
        cols = slice(128 * i, 128 * (i + 1))
        grow = jnp.where(left, decay[:, 2 * i : 2 * i + 1], decay[:, 2 * i + 1 : 2 * i + 2])
        part = fs[i // 2, :, 128 * (i % 2) : 128 * (i % 2) + 128].astype(F32)
        gate = gate_ref[:, cols].astype(F32)
        gated = (yb[:, cols] + grow * part) * (gate / (1.0 + jnp.exp(-gate)))
        yb[:, cols] = gated
        squares = squares + gated * gated
    own_sum = jnp.sum(squares, axis=1, keepdims=True)
    sq_out[...] = jnp.broadcast_to(own_sum, (TOK, 128))
    send(sq_out, sq_in, pair_s.at[10], pair_r.at[10], partner).wait_recv()
    mean = (sq_out[...] + sq_in[...]) * (1.0 / 2048)
    scale = lax.rsqrt(mean + EPSILON)
    for i in range(HEADS // 2):
        cols = slice(128 * i, 128 * (i + 1))
        ssm_out[:, cols] = (yb[:, cols] * scale * gain_ref[:, cols]).astype(BF)
    for copy in sends:
        copy.wait_send()


def shards(
    ssm_input, ssm_gate, step_size, log_decay, input_b, input_c, skip_gain, norm_gain,
    attn_queries, attn_keys, attn_values,
):
    hbm = pl.BlockSpec(memory_space=pl.ANY)
    vmem = pl.BlockSpec(memory_space=pltpu.VMEM)
    dma = pltpu.SemaphoreType.DMA
    return pl.pallas_call(
        kernel,
        out_shape=(
            jax.ShapeDtypeStruct((TOK, 1024), BF),
            jax.ShapeDtypeStruct((TOK, 512), BF),
        ),
        in_specs=[hbm] * 6 + [vmem] * 2 + [hbm] * 3,
        out_specs=(vmem, vmem),
        scratch_shapes=[
            pltpu.VMEM((TOK, 1024), BF),
            pltpu.VMEM((TOK, 1024), BF),
            pltpu.VMEM((TOK, HEADS), F32),
            pltpu.VMEM((TOK, HEADS), F32),
            pltpu.VMEM((TOK, 512), BF),
            pltpu.VMEM((16, 128), BF),
            pltpu.VMEM((2, TOK, 64), BF),
            pltpu.VMEM((2, TOK, 64), BF),
            pltpu.VMEM((NY, 2, TOK, 128), BF),
            pltpu.VMEM((NY, 2, TOK, 128), BF),
            pltpu.VMEM((NY, TOK, QW), BF),
            pltpu.VMEM((NY, 8, TOK), F32),
            pltpu.VMEM((NY, 8, TOK), F32),
            pltpu.VMEM((NZ, 32, QW), BF),
            pltpu.VMEM((NZ, 32, QW), BF),
            pltpu.VMEM((8, QW), F32),
            pltpu.VMEM((NZ, 8, QW), F32),
            pltpu.VMEM((NZ, 32, QW), BF),
            pltpu.VMEM((NZ, 32, QW), BF),
            pltpu.VMEM((NY, TOK, QW), F32),
            pltpu.VMEM((NY, TOK, QW), BF),
            pltpu.VMEM((NY, TOK, QW), BF),
            pltpu.VMEM((2, NZ, NY, TOK, 128), BF),
            pltpu.VMEM((QH, TOK, 128), F32),
            pltpu.VMEM((QH, TOK, 128), F32),
            pltpu.VMEM((QH, TOK, 128), F32),
            pltpu.VMEM((TOK, 1024), F32),
            pltpu.VMEM((TOK, 128), F32),
            pltpu.VMEM((TOK, 128), F32),
            dma((10,)),
            dma((11,)),
            dma((11,)),
            dma((5, NY)),
            dma((5, NY)),
            dma((3, NZ)),
            dma((3, NZ)),
            dma((NY,)),
            dma((NY,)),
            dma((4, NY)),
            dma((4, NY)),
            dma((3, NY)),
            dma((3, NY)),
            dma((8,)),
            dma((8,)),
        ],
        name="hybrid_mixer",
        compiler_params=pltpu.CompilerParams(
            collective_id=0, has_side_effects=True, vmem_limit_bytes=40 << 20
        ),
    )(
        ssm_input, ssm_gate, step_size, log_decay, input_b, input_c,
        skip_gain.reshape(1, HEADS), norm_gain.reshape(1, 1024),
        attn_queries, attn_keys, attn_values,
    )


def solution(mesh):
    split = P("ctx", "head")
    return jax.shard_map(
        shards,
        mesh=mesh,
        in_specs=(split,) * 6 + (P("head"), P("head")) + (split,) * 3,
        out_specs=(split, split),
        check_vma=False,
    )
```

```python
import functools
import math

import jax
import jax.numpy as jnp
from jax import lax
from jax.experimental import pallas as pl
from jax.experimental.pallas import tpu as pltpu
from jax.sharding import PartitionSpec as P

MESH = pl.DeviceIdType.MESH
BF = jnp.bfloat16
F32 = jnp.float32
HI = lax.Precision.HIGHEST

TOK = 128
NZ, NY = 8, 4
HEADS = 16
QW = 256
QH = 4
EPSILON = 1e-05
NEGATIVE = -1e30
SCALE = 1.0 / math.sqrt(128)

NT = (((1,), (1,)), ((), ()))
TN = (((0,), (0,)), ((), ()))


def dot(a, b, dims=(((1,), (0,)), ((), ())), precision=None):
    return lax.dot_general(a, b, dims, precision=precision, preferred_element_type=F32)


def kernel(
    x_hbm, gate_hbm, dt_hbm, ld_hbm, b_hbm, c_hbm, skip_ref, gain_ref, q_hbm, k_hbm, v_hbm,
    ssm_out, attn_out,
    x_ref, gate_ref, dt_ref, ld_ref, q_ref, khalf, vhalf,
    brow, crow, xrow, pk, prow, tb, zin, lam_out, lam_in, rz, rin, early, gout, fs,
    kv, m_ref, l_ref, acc_ref, yb, sq_out, sq_in,
    load_sem, pair_s, pair_r, y_s, y_r, z_s, z_r, kvy_s, kvy_r, kvp_s, kvp_r, kvm_s, kvm_r, kvh_s, kvh_r,
):
    ctx = lax.axis_index("ctx")
    head = lax.axis_index("head")
    z, y = lax.div(ctx, NY), lax.rem(ctx, NY)
    core = lax.rem(head, 2)
    partner = (ctx, head + 1 - 2 * core)
    y_peer = [None] + [(z * NY + lax.rem(y + k, NY), head) for k in range(1, NY)]
    z_peer = [None] + [(lax.rem(z + k, NZ) * NY + y, head) for k in range(1, NZ)]
    y_at = [lax.rem(y + k, NY) for k in range(NY)]
    z_at = [lax.rem(z + k, NZ) for k in range(NZ)]

    barrier = pltpu.get_barrier_semaphore()
    for peer in [partner] + y_peer[1:] + z_peer[1:]:
        pl.semaphore_signal(barrier, inc=1, device_id=peer, device_id_type=MESH)

    loads = [
        pltpu.make_async_copy(src, dst, load_sem.at[i])
        for i, (src, dst) in enumerate(
            [
                (dt_hbm, dt_ref),
                (ld_hbm, ld_ref),
                (k_hbm, khalf.at[core]),
                (v_hbm, vhalf.at[core]),
                (b_hbm, brow.at[y, core]),
                (c_hbm, crow.at[y, core]),
                (x_hbm, x_ref),
                (x_hbm.at[:, pl.ds(pl.multiple_of(y * QW, QW), QW)], xrow.at[y]),
                (q_hbm, q_ref),
                (gate_hbm, gate_ref),
            ]
        )
    ]
    for load in loads:
        load.start()

    sends = []

    def send(src, dst, s_sem, r_sem, device):
        copy = pltpu.make_async_remote_copy(
            src_ref=src, dst_ref=dst, send_sem=s_sem, recv_sem=r_sem, device_id=device, device_id_type=MESH
        )
        copy.start()
        sends.append(copy)
        return copy

    loads[0].wait()
    loads[1].wait()
    row = lax.broadcasted_iota(jnp.int32, (TOK, TOK), 0)
    col = lax.broadcasted_iota(jnp.int32, (TOK, TOK), 1)
    lower = col <= row
    tri = lower.astype(F32)
    lane = lax.broadcasted_iota(jnp.int32, (1, TOK), 1)
    left = lane < 64
    ld_t = ld_ref[...]
    cum = dot(tri, ld_t, NT, precision=HI)
    cum_t = dot(ld_t, (row <= col).astype(F32), precision=HI)
    dt_t = dt_ref[...]
    block_log = cum_t[:, TOK - 1 : TOK]
    weight_t = jnp.exp(block_log - cum_t) * dt_t
    log_t = jnp.broadcast_to(block_log, (HEADS, TOK))
    for quarter in range(NY):
        heads = slice(4 * quarter, 4 * quarter + 4)
        pk[quarter] = jnp.concatenate([weight_t[heads], log_t[heads]], axis=0)
    prow[y] = pk[y]
    for i in (2, 3, 4, 5):
        loads[i].wait()

    pl.semaphore_wait(barrier, 1 + (NY - 1) + (NZ - 1))

    pair_k = send(khalf.at[core], khalf.at[core], pair_s.at[0], pair_r.at[0], partner)
    pair_v = send(vhalf.at[core], vhalf.at[core], pair_s.at[1], pair_r.at[1], partner)
    pair_b = send(brow.at[y, core], brow.at[y, core], pair_s.at[2], pair_r.at[2], partner)
    pair_c = send(crow.at[y, core], crow.at[y, core], pair_s.at[3], pair_r.at[3], partner)
    y_pk, y_b, y_x, y_c = [None], [None], [None], [None]
    for k in range(1, NY):
        y_b.append(send(brow.at[y, core], brow.at[y, core], y_s.at[0, k], y_r.at[0, k], y_peer[k]))
        y_pk.append(send(pk.at[y_at[k]], prow.at[y], y_s.at[1, k], y_r.at[1, k], y_peer[k]))
    for k in range(1, NY):
        quarter = x_hbm.at[:, pl.ds(pl.multiple_of(y_at[k] * QW, QW), QW)]
        y_x.append(send(quarter, xrow.at[y], y_s.at[2, k], y_r.at[2, k], y_peer[k]))

    pair_k.wait_recv()
    pair_v.wait_recv()
    kv[0, 0, 0] = khalf[...].reshape(128, TOK)
    kv[1, 0, 0] = vhalf[...].reshape(128, TOK).T

    plus, minus, row_kv, hand = {}, {}, {}, {}

    def send_plus(s, k):
        plus[s, k] = send(
            kv.at[core, s, k], kv.at[core, s + 1, k], kvp_s.at[s, k], kvp_r.at[s, k], z_peer[1]
        )

    def send_minus(s, k):
        minus[s, k] = send(
            kv.at[core, (NZ - s) % NZ, k], kv.at[core, 7 - s, k], kvm_s.at[s, k], kvm_r.at[s, k], z_peer[NZ - 1]
        )

    def hand_over(i, slot, first):
        part = kv.at[core, slot, pl.ds(first, NY - first)]
        hand[slot] = send(part, part, kvh_s.at[i], kvh_r.at[i], partner)

    def pump(s, blocks):
        for k in blocks:
            plus[s, k].wait_recv()
            if s < 3:
                send_plus(s + 1, k)
            if s < 3:
                minus[s, k].wait_recv()
                if s < 2:
                    send_minus(s + 1, k)

    def hand_rows(s):
        hand_over(1 + 2 * s, s + 1, 0)
        if s < 3:
            hand_over(2 + 2 * s, 7 - s, 0)

    send_plus(0, 0)
    send_minus(0, 0)
    for k in range(1, NY):
        row_kv[k] = send(kv.at[core, 0, 0], kv.at[core, 0, NY - k], kvy_s.at[k], kvy_r.at[k], y_peer[k])

    loads[8].wait()

    def attend(keys, values, first=False):
        for h in range(QH):
            query = q_ref[:, h * 128 : (h + 1) * 128]
            scores = jnp.concatenate([dot(query, part) for part in keys], axis=1)
            if first:
                scores = jnp.where(lower, scores, NEGATIVE)
                top = jnp.max(scores, axis=1, keepdims=True)
                weights = jnp.exp((scores - top) * SCALE)
                total = jnp.sum(weights, axis=1, keepdims=True)
                mixed = dot(weights.astype(BF), values)
            else:
                before = m_ref[h][:, :1]
                top = jnp.maximum(before, jnp.max(scores, axis=1, keepdims=True))
                factor = jnp.exp((before - top) * SCALE)
                weights = jnp.exp((scores - top) * SCALE)
                total = l_ref[h][:, :1] * factor + jnp.sum(weights, axis=1, keepdims=True)
                mixed = acc_ref[h] * factor + dot(weights.astype(BF), values)
            m_ref[h] = jnp.broadcast_to(top, (TOK, 128))
            l_ref[h] = jnp.broadcast_to(total, (TOK, 128))
            acc_ref[h] = mixed

    def attend_row(slot):
        @pl.when(z >= slot)
        def _():
            attend([kv[0, slot, k] for k in range(NY)], kv[1, slot].reshape(NY * TOK, 128))

    attend([kv[0, 0, 0]], kv[1, 0, 0], first=True)

    pair_b.wait_recv()
    pair_c.wait_recv()
    loads[6].wait()
    inner = dot(crow[y, 0], brow[y, 0], NT) + dot(crow[y, 1], brow[y, 1], NT)
    for i in range(HEADS // 2):
        cols = slice(128 * i, 128 * (i + 1))
        x_two = x_ref[:, cols]
        parts = []
        for h in (2 * i, 2 * i + 1):
            gap = jnp.where(lower, cum[:, h : h + 1] - cum_t[h : h + 1, :], NEGATIVE)
            mix = (inner * jnp.exp(gap) * dt_t[h : h + 1, :]).astype(BF)
            parts.append(dot(mix, x_two))
        gain = jnp.where(left, skip_ref[:, 2 * i : 2 * i + 1], skip_ref[:, 2 * i + 1 : 2 * i + 2])
        yb[:, cols] = jnp.where(left, parts[0], parts[1]) + gain * x_two.astype(F32)

    pump(0, [0])

    hand_b = [None]
    for k in range(1, NY):
        y_b[k].wait_recv()
        part = brow.at[y_at[NY - k], core]
        hand_b.append(send(part, part, pair_s.at[3 + k], pair_r.at[3 + k], partner))
    pump(1, [0])
    loads[7].wait()
    for k in range(1, NY):
        y_pk[k].wait_recv()
        y_x[k].wait_recv()
    for k in range(1, NY):
        hand_b[k].wait_recv()
    packed = prow[...]
    columns = packed.reshape(NY * 8, TOK).T

    def two_by_two(parts):
        return jnp.concatenate(
            [jnp.where(left, parts[0], parts[1]), jnp.where(left, parts[2], parts[3])], axis=1
        )

    logs = [two_by_two([packed[j, 4 + i : 5 + i] for i in range(4)]) for j in range(NY)]
    lam_out[...] = jnp.broadcast_to(logs[0] + logs[1] + logs[2] + logs[3], (8, QW))
    z_lam = [None]
    for k in range(1, NZ):
        z_lam.append(send(lam_out, lam_in.at[z], z_s.at[0, k], z_r.at[0, k], z_peer[k]))
    lam_in[z] = lam_out[...]
    state = None
    priors = [None]
    for j in range(NY):
        weight = two_by_two([columns[:, 8 * j + i : 8 * j + i + 1] for i in range(4)])
        weighted = (xrow[j].astype(F32) * weight).astype(BF)
        own = jnp.concatenate([dot(brow[j, 0], weighted, TN), dot(brow[j, 1], weighted, TN)], axis=0)
        state = own if state is None else state * jnp.exp(logs[j]) + own
        priors.append(state)
    tb[...] = state.astype(BF).reshape(NZ, 32, QW)
    z_one = [None]
    for k in range(1, NZ):
        z_one.append(send(tb.at[z_at[k]], zin.at[z], z_s.at[1, k], z_r.at[1, k], z_peer[k]))
    zin[z] = tb[z]
    for k in range(1, NY):
        y_c.append(send(crow.at[y, core], crow.at[y, core], y_s.at[3, k], y_r.at[3, k], y_peer[k]))

    pump(2, [0])
    for k in range(1, NY):
        row_kv[k].wait_recv()
        send_plus(0, NY - k)
        send_minus(0, NY - k)
    hand_over(0, 0, 1)
    pump(3, [0])

    hand_c = [None]
    for k in range(1, NY):
        y_c[k].wait_recv()
        part = crow.at[y_at[NY - k], core]
        hand_c.append(send(part, part, pair_s.at[6 + k], pair_r.at[6 + k], partner))
    for k in range(1, NY):
        hand_c[k].wait_recv()
    for j in range(1, NY):
        prior = priors[j].astype(BF)
        early[j] = dot(crow[j, 0], prior[:128]) + dot(crow[j, 1], prior[128:])

    for k in range(1, NZ):
        z_lam[k].wait_recv()
        z_one[k].wait_recv()
    state = jnp.zeros((32, QW), F32)
    for r in range(NZ):
        rz[r] = state.astype(BF)
        if r < NZ - 1:
            state = state * jnp.exp(lam_in[r, 0:1]) + zin[r].astype(F32)
    z_two = [None]
    for k in range(1, NZ):
        z_two.append(send(rz.at[z_at[k]], rin.at[z], z_s.at[2, k], z_r.at[2, k], z_peer[k]))
    rin[z] = rz[z]

    hand[0].wait_recv()
    for k in range(1, NY):

        @pl.when(y + k >= NY)
        def _():
            attend([kv[0, 0, k]], kv[1, 0, k])

    pump(0, [1, 2, 3])
    hand_rows(0)
    pump(1, [1, 2, 3])
    hand_rows(1)
    hand[1].wait_recv()
    attend_row(1)

    for k in range(1, NZ):
        z_two[k].wait_recv()
    entering = rin[...].reshape(QW, QW)
    before = jnp.zeros((1, QW), F32)
    for j in range(NY):
        part = dot(crow[j, 0], entering[:128]) + dot(crow[j, 1], entering[128:])
        if j > 0:
            before = before + logs[j - 1]
            part = part * jnp.exp(before) + early[j]
        gout[j] = part.astype(BF)
    y_out = [None]
    for k in range(1, NY):
        y_out.append(send(gout.at[y_at[k]], fs.at[y], y_s.at[4, k], y_r.at[4, k], y_peer[k]))
    fs[y] = gout[y]

    pump(2, [1, 2, 3])
    hand_rows(2)
    hand[7].wait_recv()
    attend_row(7)
    pump(3, [1, 2, 3])
    hand_rows(3)
    for slot in (2, 6, 3, 5, 4):
        hand[slot].wait_recv()
        attend_row(slot)
    for h in range(QH):
        attn_out[:, h * 128 : (h + 1) * 128] = (acc_ref[h] / l_ref[h]).astype(BF)

    for k in range(1, NY):
        y_out[k].wait_recv()
    loads[9].wait()
    decay = jnp.exp(cum)
    squares = jnp.zeros((TOK, 128), F32)
    for i in range(HEADS // 2):
        cols = slice(128 * i, 128 * (i + 1))
        grow = jnp.where(left, decay[:, 2 * i : 2 * i + 1], decay[:, 2 * i + 1 : 2 * i + 2])
        part = fs[i // 2, :, 128 * (i % 2) : 128 * (i % 2) + 128].astype(F32)
        gate = gate_ref[:, cols].astype(F32)
        gated = (yb[:, cols] + grow * part) * (gate / (1.0 + jnp.exp(-gate)))
        yb[:, cols] = gated
        squares = squares + gated * gated
    own_sum = jnp.sum(squares, axis=1, keepdims=True)
    sq_out[...] = jnp.broadcast_to(own_sum, (TOK, 128))
    send(sq_out, sq_in, pair_s.at[10], pair_r.at[10], partner).wait_recv()
    mean = (sq_out[...] + sq_in[...]) * (1.0 / 2048)
    scale = lax.rsqrt(mean + EPSILON)
    for i in range(HEADS // 2):
        cols = slice(128 * i, 128 * (i + 1))
        ssm_out[:, cols] = (yb[:, cols] * scale * gain_ref[:, cols]).astype(BF)
    for copy in sends:
        copy.wait_send()


def shards(
    ssm_input, ssm_gate, step_size, log_decay, input_b, input_c, skip_gain, norm_gain,
    attn_queries, attn_keys, attn_values,
):
    hbm = pl.BlockSpec(memory_space=pltpu.HBM)
    vmem = pl.BlockSpec(memory_space=pltpu.VMEM)
    dma = pltpu.SemaphoreType.DMA
    return pl.pallas_call(
        kernel,
        out_shape=(
            jax.ShapeDtypeStruct((TOK, 1024), BF),
            jax.ShapeDtypeStruct((TOK, 512), BF),
        ),
        in_specs=[hbm] * 6 + [vmem] * 2 + [hbm] * 3,
        out_specs=(vmem, vmem),
        scratch_shapes=[
            pltpu.VMEM((TOK, 1024), BF),
            pltpu.VMEM((TOK, 1024), BF),
            pltpu.VMEM((HEADS, TOK), F32),
            pltpu.VMEM((HEADS, TOK), F32),
            pltpu.VMEM((TOK, 512), BF),
            pltpu.VMEM((2, 64, TOK), BF),
            pltpu.VMEM((2, 64, TOK), BF),
            pltpu.VMEM((NY, 2, TOK, 128), BF),
            pltpu.VMEM((NY, 2, TOK, 128), BF),
            pltpu.VMEM((NY, TOK, QW), BF),
            pltpu.VMEM((NY, 8, TOK), F32),
            pltpu.VMEM((NY, 8, TOK), F32),
            pltpu.VMEM((NZ, 32, QW), BF),
            pltpu.VMEM((NZ, 32, QW), BF),
            pltpu.VMEM((8, QW), F32),
            pltpu.VMEM((NZ, 8, QW), F32),
            pltpu.VMEM((NZ, 32, QW), BF),
            pltpu.VMEM((NZ, 32, QW), BF),
            pltpu.VMEM((NY, TOK, QW), F32),
            pltpu.VMEM((NY, TOK, QW), BF),
            pltpu.VMEM((NY, TOK, QW), BF),
            pltpu.VMEM((2, NZ, NY, TOK, 128), BF),
            pltpu.VMEM((QH, TOK, 128), F32),
            pltpu.VMEM((QH, TOK, 128), F32),
            pltpu.VMEM((QH, TOK, 128), F32),
            pltpu.VMEM((TOK, 1024), F32),
            pltpu.VMEM((TOK, 128), F32),
            pltpu.VMEM((TOK, 128), F32),
            dma((10,)),
            dma((11,)),
            dma((11,)),
            dma((5, NY)),
            dma((5, NY)),
            dma((3, NZ)),
            dma((3, NZ)),
            dma((NY,)),
            dma((NY,)),
            dma((4, NY)),
            dma((4, NY)),
            dma((3, NY)),
            dma((3, NY)),
            dma((8,)),
            dma((8,)),
        ],
        name="hybrid_mixer",
        compiler_params=pltpu.CompilerParams(
            collective_id=0, has_side_effects=True, vmem_limit_bytes=56 << 20
        ),
    )(
        ssm_input, ssm_gate, step_size.T, log_decay.T, input_b, input_c,
        skip_gain.reshape(1, HEADS), norm_gain.reshape(1, 1024),
        attn_queries, attn_keys.T, attn_values.T,
    )


def solution(mesh):
    split = P("ctx", "head")
    return jax.shard_map(
        shards,
        mesh=mesh,
        in_specs=(split,) * 6 + (P("head"), P("head")) + (split,) * 3,
        out_specs=(split, split),
        check_vma=False,
    )
```

```python
import functools
import math

import jax
import jax.numpy as jnp
from jax import lax
from jax.experimental import pallas as pl
from jax.experimental.pallas import tpu as pltpu
from jax.sharding import PartitionSpec as P

MESH = pl.DeviceIdType.MESH
BF = jnp.bfloat16
F32 = jnp.float32
HI = lax.Precision.HIGHEST

TOK = 128
NZ, NY = 8, 4
HEADS = 16
QW = 256
QH = 4
EPSILON = 1e-05
NEGATIVE = -1e30
SCALE = math.log2(math.e) / math.sqrt(128)

NT = (((1,), (1,)), ((), ()))
TN = (((0,), (0,)), ((), ()))


def dot(a, b, dims=(((1,), (0,)), ((), ())), precision=None):
    return lax.dot_general(a, b, dims, precision=precision, preferred_element_type=F32)


class Transfer:
    def __init__(self, copy, sent=None, received=None):
        self.copy, self.sent, self.received = copy, sent, received

    @staticmethod
    def under(condition, action):
        if condition is None:
            action()
        else:
            pl.when(condition)(lambda: action())

    def start(self):
        self.under(self.sent, self.copy.start)
        return self

    def wait_recv(self):
        self.under(self.received, self.copy.wait_recv)

    def wait_send(self):
        self.under(self.sent, self.copy.wait_send)


def kernel(
    x_hbm, gate_hbm, dt_hbm, ld_hbm, b_hbm, c_hbm, skip_ref, gain_ref, q_hbm, k_hbm, v_hbm,
    ssm_out, attn_out,
    x_ref, gate_ref, dt_ref, ld_ref, q_ref, khalf, vhalf,
    brow, crow, xrow, pk, prow, change, prior, rz, rin, early, gout, fs,
    kv, m_ref, l_ref, acc_ref, stacked, yb, sq_out, sq_in,
    load_sem, pair_s, pair_r, y_s, y_r, z_s, z_r, kvy_s, kvy_r, kvp_s, kvp_r, kvm_s, kvm_r, kvh_s, kvh_r, ready,
):
    ctx = lax.axis_index("ctx")
    head = lax.axis_index("head")
    z, y = lax.div(ctx, NY), lax.rem(ctx, NY)
    core = lax.rem(head, 2)
    partner = (ctx, head + 1 - 2 * core)
    y_peer = [None] + [(z * NY + lax.rem(y + k, NY), head) for k in range(1, NY)]
    next_row = (lax.rem(z + 1, NZ) * NY + y, head)
    last_row = (lax.rem(z + NZ - 1, NZ) * NY + y, head)
    y_at = [lax.rem(y + k, NY) for k in range(NY)]

    barrier = pltpu.get_barrier_semaphore()

    def greet(peer):
        pl.semaphore_signal(barrier, inc=1, device_id=peer, device_id_type=MESH)

    for peer in [partner] + y_peer[1:]:
        greet(peer)
    pl.when(z > 0)(lambda: greet(last_row))
    pl.when(z < NZ - 1)(lambda: greet(next_row))
    for s in (5, 6, 7):

        @pl.when(z + s < NZ)
        def _():
            greet((lax.rem(z + s, NZ) * NY + y, head))


    loads = [
        pltpu.make_async_copy(src, dst, load_sem.at[i])
        for i, (src, dst) in enumerate(
            [
                (dt_hbm, dt_ref),
                (ld_hbm, ld_ref),
                (k_hbm, khalf.at[core]),
                (v_hbm, vhalf.at[core]),
                (b_hbm, brow.at[y, core]),
                (c_hbm, crow.at[y, core]),
                (x_hbm, x_ref),
                (x_hbm.at[:, pl.ds(pl.multiple_of(y * QW, QW), QW)], xrow.at[y]),
                (q_hbm, q_ref),
                (gate_hbm, gate_ref),
            ]
        )
    ]
    for load in loads:
        load.start()

    sends = []

    def plan(src, dst, s_sem, r_sem, device, sent=None, received=None):
        copy = Transfer(
            pltpu.make_async_remote_copy(
                src_ref=src, dst_ref=dst, send_sem=s_sem, recv_sem=r_sem, device_id=device, device_id_type=MESH
            ),
            sent,
            received,
        )
        sends.append(copy)
        return copy

    def send(*args, **kwargs):
        return plan(*args, **kwargs).start()

    y_b, y_pk, y_x, y_c, y_kv, y_out = [None], [None], [None], [None], [None], [None]
    hand_b, hand_c = [None], [None]
    for k in range(1, NY):
        own_b, own_c = brow.at[y, core], crow.at[y, core]
        y_b.append(plan(own_b, own_b, y_s.at[0, k], y_r.at[0, k], y_peer[k]))
        y_pk.append(plan(pk.at[y_at[k]], prow.at[y], y_s.at[1, k], y_r.at[1, k], y_peer[k]))
        quarter = x_hbm.at[:, pl.ds(pl.multiple_of(y_at[k] * QW, QW), QW)]
        y_x.append(plan(quarter, xrow.at[y], y_s.at[2, k], y_r.at[2, k], y_peer[k]))
        y_c.append(plan(own_c, own_c, y_s.at[3, k], y_r.at[3, k], y_peer[k]))
        y_out.append(plan(gout.at[y_at[k]], fs.at[y], y_s.at[4, k], y_r.at[4, k], y_peer[k]))
        y_kv.append(plan(kv.at[core, 0, 0], kv.at[core, 0, NY - k], kvy_s.at[k], kvy_r.at[k], y_peer[k]))
        came_b, came_c = brow.at[y_at[NY - k], core], crow.at[y_at[NY - k], core]
        hand_b.append(plan(came_b, came_b, pair_s.at[3 + k], pair_r.at[3 + k], partner))
        hand_c.append(plan(came_c, came_c, pair_s.at[6 + k], pair_r.at[6 + k], partner))
    plus = {
        (s, k): plan(
            kv.at[core, s, k], kv.at[core, s + 1, k], kvp_s.at[s, k], kvp_r.at[s, k], next_row,
            (z >= s) & (z < NZ - 1), z >= s + 1,
        )
        for s in range(4)
        for k in range(NY)
    }
    far = {
        s: plan(
            kv.at[core, 0], kv.at[core, s], kvm_s.at[s - 5], kvm_r.at[s - 5], (lax.rem(z + s, NZ) * NY + y, head),
            z + s < NZ, z >= s,
        )
        for s in (5, 6, 7)
    }
    hand = []
    for slot in range(NZ):
        part = kv.at[core, slot, pl.ds(1, NY - 1)] if slot == 0 else kv.at[core, slot]
        used = None if slot == 0 else z >= slot
        hand.append(plan(part, part, kvh_s.at[slot], kvh_r.at[slot], partner, used, used))
    z_chain = [
        plan(rz.at[i], rin.at[i], z_s.at[i], z_r.at[i], next_row, z < NZ - 1, z > 0) for i in range(NZ)
    ]
    swap = plan(sq_out, sq_in, pair_s.at[10], pair_r.at[10], partner)

    loads[0].wait()
    loads[1].wait()
    row = lax.broadcasted_iota(jnp.int32, (TOK, TOK), 0)
    col = lax.broadcasted_iota(jnp.int32, (TOK, TOK), 1)
    lower = col <= row
    lane = lax.broadcasted_iota(jnp.int32, (1, TOK), 1)
    left = lane < 64
    ld_t = ld_ref[...]
    cum = dot(lower.astype(F32), ld_t, NT, precision=HI)
    cum_t = dot(ld_t, (row <= col).astype(F32), precision=HI)
    dt_t = dt_ref[...]
    block_log = cum_t[:, TOK - 1 : TOK]
    weight_t = jnp.exp(block_log - cum_t) * dt_t
    log_t = jnp.broadcast_to(block_log, (HEADS, TOK))
    for quarter in range(NY):
        heads = slice(4 * quarter, 4 * quarter + 4)
        pk[quarter] = jnp.concatenate([weight_t[heads], log_t[heads]], axis=0)
    prow[y] = pk[y]
    for i in (2, 3, 4, 5):
        loads[i].wait()
    @pl.when(z == 0)
    def _():
        rin[...] = jnp.zeros_like(rin)

    pl.semaphore_wait(barrier, NY + jnp.where(z > 0, 1, 0) + jnp.where(z < NZ - 1, 1, 0) + jnp.maximum(z - 4, 0))

    for s in (5, 6, 7):

        @pl.when(z >= s)
        def _():
            pl.semaphore_signal(
                ready.at[s - 5], inc=1, device_id=(lax.rem(z + NZ - s, NZ) * NY + y, head), device_id_type=MESH
            )

    pair_k = send(khalf.at[core], khalf.at[core], pair_s.at[0], pair_r.at[0], partner)
    pair_v = send(vhalf.at[core], vhalf.at[core], pair_s.at[1], pair_r.at[1], partner)
    pair_b = send(brow.at[y, core], brow.at[y, core], pair_s.at[2], pair_r.at[2], partner)
    pair_c = send(crow.at[y, core], crow.at[y, core], pair_s.at[3], pair_r.at[3], partner)
    for k in range(1, NY):
        y_b[k].start()
        y_pk[k].start()
    for k in range(1, NY):
        y_x[k].start()

    pair_k.wait_recv()
    pair_v.wait_recv()
    kv[0, 0, 0] = khalf[...].reshape(128, TOK)
    kv[1, 0, 0] = vhalf[...].reshape(128, TOK).T

    def pump(s, blocks):
        for k in blocks:
            plus[s, k].wait_recv()
            if s < 3:
                plus[s + 1, k].start()

    plus[0, 0].start()

    loads[8].wait()

    for h in range(QH):
        stacked[h * TOK : (h + 1) * TOK] = q_ref[:, h * 128 : (h + 1) * 128]

    def attend(keys, values, first=False):
        for h in range(QH):
            rows = slice(h * TOK, (h + 1) * TOK)
            scores = [dot(stacked[rows], part) for part in keys]
            if first:
                scores = [jnp.where(lower, scores[0], NEGATIVE)]
            top = functools.reduce(jnp.maximum, scores)
            top = jnp.broadcast_to(jnp.max(top, axis=1, keepdims=True), (TOK, 128))
            if not first:
                before = m_ref[rows]
                top = jnp.maximum(before, top)
                factor = jnp.exp2((before - top) * SCALE)
            weights = [jnp.exp2((part - top) * SCALE) for part in scores]
            total = functools.reduce(jnp.add, weights)
            mixed = dot(jnp.concatenate([part.astype(BF) for part in weights], axis=1), values)
            m_ref[rows] = top
            l_ref[rows] = total if first else l_ref[rows] * factor + total
            acc_ref[rows] = mixed if first else acc_ref[rows] * factor + mixed

    def attend_row(slot):
        hand[slot].wait_recv()

        @pl.when(z >= slot)
        def _():
            attend([kv[0, slot, k] for k in range(NY)], kv[1, slot].reshape(NY * TOK, 128))

    attend([kv[0, 0, 0]], kv[1, 0, 0], first=True)
    pump(0, [0])

    pair_b.wait_recv()
    pair_c.wait_recv()
    loads[6].wait()
    inner = dot(crow[y, 0], brow[y, 0], NT) + dot(crow[y, 1], brow[y, 1], NT)
    for i in range(HEADS // 2):
        cols = slice(128 * i, 128 * (i + 1))
        x_two = x_ref[:, cols]
        parts = []
        for h in (2 * i, 2 * i + 1):
            gap = jnp.where(lower, cum[:, h : h + 1] - cum_t[h : h + 1, :], NEGATIVE)
            mix = (inner * jnp.exp(gap) * dt_t[h : h + 1, :]).astype(BF)
            parts.append(dot(mix, x_two))
        gain = jnp.where(left, skip_ref[:, 2 * i : 2 * i + 1], skip_ref[:, 2 * i + 1 : 2 * i + 2])
        yb[:, cols] = jnp.where(left, parts[0], parts[1]) + gain * x_two.astype(F32)
        if i == 3:
            pump(1, [0])
    pump(2, [0])

    for k in range(1, NY):
        y_b[k].wait_recv()
        hand_b[k].start()
    loads[7].wait()
    for k in range(1, NY):
        y_pk[k].wait_recv()
        y_x[k].wait_recv()
    for k in range(1, NY):
        y_kv[k].start()
    for k in range(1, NY):
        y_c[k].start()
    for k in range(1, NY):
        hand_b[k].wait_recv()
    packed = prow[...]
    columns = packed.reshape(NY * 8, TOK).T

    def two_by_two(parts):
        return jnp.concatenate(
            [jnp.where(left, parts[0], parts[1]), jnp.where(left, parts[2], parts[3])], axis=1
        )

    logs = [two_by_two([packed[j, 4 + i : 5 + i] for i in range(4)]) for j in range(NY)]
    row_decay = jnp.exp(logs[0] + logs[1] + logs[2] + logs[3])
    state = None
    for j in range(NY):
        weight = two_by_two([columns[:, 8 * j + i : 8 * j + i + 1] for i in range(4)])
        weighted = (xrow[j].astype(F32) * weight).astype(BF)
        own = jnp.concatenate([dot(brow[j, 0], weighted, TN), dot(brow[j, 1], weighted, TN)], axis=0)
        state = own if state is None else state * jnp.exp(logs[j]) + own
        if j < NY - 1:
            prior[j + 1] = state.astype(BF)
    change[...] = state.reshape(NZ, 32, QW)
    pump(3, [0])

    def share_row():
        for k in range(1, NY):
            y_kv[k].wait_recv()
            plus[0, NY - k].start()
        hand[0].start()

        for s in (5, 6, 7):

            @pl.when(z + s < NZ)
            def _():
                pl.semaphore_wait(ready.at[s - 5], 1)

            far[s].start()


    def row_part():
        for k in range(1, NY):
            y_c[k].wait_recv()
            hand_c[k].start()
        for k in range(1, NY):
            hand_c[k].wait_recv()
        for j in range(1, NY):
            early[j] = dot(crow[j, 0], prior[j, :128]) + dot(crow[j, 1], prior[j, 128:])

    def near_rows():
        pump(0, [1, 2, 3])
        hand[1].start()
        hand[0].wait_recv()
        for k in range(1, NY):

            @pl.when(y + k >= NY)
            def _():
                attend([kv[0, 0, k]], kv[1, 0, k])

        pump(1, [1, 2, 3])
        hand[2].start()
        attend_row(1)

    late = z >= 7

    @pl.when(z >= 4)
    def _():
        share_row()
        row_part()

    pl.when(late)(near_rows)
    for i in range(NZ):
        z_chain[i].wait_recv()
        rz[i] = (rin[i].astype(F32) * row_decay + change[i]).astype(BF)
        z_chain[i].start()

    @pl.when(z < 4)
    def _():
        share_row()
        row_part()

    entering = rin[...].reshape(QW, QW)
    before = jnp.zeros((1, QW), F32)
    for j in range(NY):
        part = dot(crow[j, 0], entering[:128]) + dot(crow[j, 1], entering[128:])
        if j > 0:
            before = before + logs[j - 1]
            part = part * jnp.exp(before) + early[j]
        gout[j] = part.astype(BF)
    for k in range(1, NY):
        y_out[k].start()
    fs[y] = gout[y]

    pl.when(~late)(near_rows)
    pump(2, [1, 2, 3])
    hand[3].start()
    attend_row(2)
    pump(3, [1, 2, 3])
    hand[4].start()
    for slot in (7, 6, 5):
        far[slot].wait_recv()
        hand[slot].start()
    for slot in (3, 4, 7, 6, 5):
        attend_row(slot)
    for h in range(QH):
        rows = slice(h * TOK, (h + 1) * TOK)
        attn_out[:, h * 128 : (h + 1) * 128] = (acc_ref[rows] / jnp.sum(l_ref[rows], axis=1, keepdims=True)).astype(BF)

    for k in range(1, NY):
        y_out[k].wait_recv()
    loads[9].wait()
    decay = jnp.exp(cum)
    squares = jnp.zeros((TOK, 128), F32)
    for i in range(HEADS // 2):
        cols = slice(128 * i, 128 * (i + 1))
        grow = jnp.where(left, decay[:, 2 * i : 2 * i + 1], decay[:, 2 * i + 1 : 2 * i + 2])
        part = fs[i // 2, :, 128 * (i % 2) : 128 * (i % 2) + 128].astype(F32)
        gate = gate_ref[:, cols].astype(F32)
        gated = (yb[:, cols] + grow * part) * (gate / (1.0 + jnp.exp(-gate)))
        yb[:, cols] = gated
        squares = squares + gated * gated
    own_sum = jnp.sum(squares, axis=1, keepdims=True)
    sq_out[...] = jnp.broadcast_to(own_sum, (TOK, 128))
    swap.start()
    swap.wait_recv()
    mean = (sq_out[...] + sq_in[...]) * (1.0 / 2048)
    scale = lax.rsqrt(mean + EPSILON)
    for i in range(HEADS // 2):
        cols = slice(128 * i, 128 * (i + 1))
        ssm_out[:, cols] = (yb[:, cols] * scale * gain_ref[:, cols]).astype(BF)
    for copy in sends:
        copy.wait_send()


def shards(
    ssm_input, ssm_gate, step_size, log_decay, input_b, input_c, skip_gain, norm_gain,
    attn_queries, attn_keys, attn_values,
):
    hbm = pl.BlockSpec(memory_space=pltpu.HBM)
    vmem = pl.BlockSpec(memory_space=pltpu.VMEM)
    dma = pltpu.SemaphoreType.DMA
    return pl.pallas_call(
        kernel,
        out_shape=(
            jax.ShapeDtypeStruct((TOK, 1024), BF),
            jax.ShapeDtypeStruct((TOK, 512), BF),
        ),
        in_specs=[hbm] * 6 + [vmem] * 2 + [hbm] * 3,
        out_specs=(vmem, vmem),
        scratch_shapes=[
            pltpu.VMEM((TOK, 1024), BF),
            pltpu.VMEM((TOK, 1024), BF),
            pltpu.VMEM((HEADS, TOK), F32),
            pltpu.VMEM((HEADS, TOK), F32),
            pltpu.VMEM((TOK, 512), BF),
            pltpu.VMEM((2, 64, TOK), BF),
            pltpu.VMEM((2, 64, TOK), BF),
            pltpu.VMEM((NY, 2, TOK, 128), BF),
            pltpu.VMEM((NY, 2, TOK, 128), BF),
            pltpu.VMEM((NY, TOK, QW), BF),
            pltpu.VMEM((NY, 8, TOK), F32),
            pltpu.VMEM((NY, 8, TOK), F32),
            pltpu.VMEM((NZ, 32, QW), F32),
            pltpu.VMEM((NY, QW, QW), BF),
            pltpu.VMEM((NZ, 32, QW), BF),
            pltpu.VMEM((NZ, 32, QW), BF),
            pltpu.VMEM((NY, TOK, QW), F32),
            pltpu.VMEM((NY, TOK, QW), BF),
            pltpu.VMEM((NY, TOK, QW), BF),
            pltpu.VMEM((2, NZ, NY, TOK, 128), BF),
            pltpu.VMEM((QH * TOK, 128), F32),
            pltpu.VMEM((QH * TOK, 128), F32),
            pltpu.VMEM((QH * TOK, 128), F32),
            pltpu.VMEM((QH * TOK, 128), BF),
            pltpu.VMEM((TOK, 1024), F32),
            pltpu.VMEM((TOK, 128), F32),
            pltpu.VMEM((TOK, 128), F32),
            dma((10,)),
            dma((11,)),
            dma((11,)),
            dma((5, NY)),
            dma((5, NY)),
            dma((NZ,)),
            dma((NZ,)),
            dma((NY,)),
            dma((NY,)),
            dma((4, NY)),
            dma((4, NY)),
            dma((3,)),
            dma((3,)),
            dma((8,)),
            dma((8,)),
            pltpu.SemaphoreType.REGULAR((3,)),
        ],
        name="hybrid_mixer",
        compiler_params=pltpu.CompilerParams(
            collective_id=0, has_side_effects=True, vmem_limit_bytes=56 << 20
        ),
    )(
        ssm_input, ssm_gate, step_size.T, log_decay.T, input_b, input_c,
        skip_gain.reshape(1, HEADS), norm_gain.reshape(1, 1024),
        attn_queries, attn_keys.T, attn_values.T,
    )


def solution(mesh):
    split = P("ctx", "head")
    return jax.shard_map(
        shards,
        mesh=mesh,
        in_specs=(split,) * 6 + (P("head"), P("head")) + (split,) * 3,
        out_specs=(split, split),
        check_vma=False,
    )
```

```python
import functools
import math

import jax
import jax.numpy as jnp
from jax import lax
from jax.experimental import pallas as pl
from jax.experimental.pallas import tpu as pltpu
from jax.sharding import PartitionSpec as P

MESH = pl.DeviceIdType.MESH
BF = jnp.bfloat16
F32 = jnp.float32
HI = lax.Precision.HIGHEST

TOK = 128
NZ, NY = 8, 4
HEADS = 16
QW = 256
QH = 4
EPSILON = 1e-05
NEGATIVE = -1e30
SCALE = math.log2(math.e) / math.sqrt(128)

NT = (((1,), (1,)), ((), ()))
TN = (((0,), (0,)), ((), ()))


def dot(a, b, dims=(((1,), (0,)), ((), ())), precision=None):
    return lax.dot_general(a, b, dims, precision=precision, preferred_element_type=F32)


class Transfer:
    def __init__(self, copy, sent=None, received=None):
        self.copy, self.sent, self.received = copy, sent, received

    @staticmethod
    def under(condition, action):
        if condition is None:
            action()
        else:
            pl.when(condition)(lambda: action())

    def start(self):
        self.under(self.sent, self.copy.start)
        return self

    def wait_recv(self):
        self.under(self.received, self.copy.wait_recv)

    def wait_send(self):
        self.under(self.sent, self.copy.wait_send)


def kernel(
    x_hbm, gate_hbm, dt_hbm, ld_hbm, b_hbm, c_hbm, skip_ref, gain_ref, q_hbm, k_hbm, v_hbm,
    ssm_out, attn_out,
    x_ref, gate_ref, dt_ref, ld_ref, q_ref, khalf, vhalf,
    brow, crow, xrow, pk, prow, change, prior, rz, rin, early, gout, fs,
    kv, m_ref, l_ref, acc_ref, stacked, yb, open_gate, sq_out, sq_in,
    load_sem, pair_s, pair_r, y_s, y_r, z_s, z_r, kvy_s, kvy_r, kvp_s, kvp_r, kvm_s, kvm_r, kvh_s, kvh_r, ready,
):
    ctx = lax.axis_index("ctx")
    head = lax.axis_index("head")
    z, y = lax.div(ctx, NY), lax.rem(ctx, NY)
    core = lax.rem(head, 2)
    partner = (ctx, head + 1 - 2 * core)
    y_peer = [None] + [(z * NY + lax.rem(y + k, NY), head) for k in range(1, NY)]
    next_row = (lax.rem(z + 1, NZ) * NY + y, head)
    last_row = (lax.rem(z + NZ - 1, NZ) * NY + y, head)
    y_at = [lax.rem(y + k, NY) for k in range(NY)]

    barrier = pltpu.get_barrier_semaphore()

    def greet(peer):
        pl.semaphore_signal(barrier, inc=1, device_id=peer, device_id_type=MESH)

    for peer in [partner] + y_peer[1:]:
        greet(peer)
    pl.when(z > 0)(lambda: greet(last_row))
    pl.when(z < NZ - 1)(lambda: greet(next_row))
    for s in (5, 6, 7):

        @pl.when(z + s < NZ)
        def _():
            greet((lax.rem(z + s, NZ) * NY + y, head))


    loads = [
        pltpu.make_async_copy(src, dst, load_sem.at[i])
        for i, (src, dst) in enumerate(
            [
                (dt_hbm, dt_ref),
                (ld_hbm, ld_ref),
                (k_hbm, khalf.at[core]),
                (v_hbm, vhalf.at[core]),
                (b_hbm, brow.at[y, core]),
                (c_hbm, crow.at[y, core]),
                (x_hbm, x_ref),
                (x_hbm.at[:, pl.ds(pl.multiple_of(y * QW, QW), QW)], xrow.at[y]),
                (q_hbm, q_ref),
                (gate_hbm, gate_ref),
            ]
        )
    ]
    for load in loads:
        load.start()

    sends = []

    def plan(src, dst, s_sem, r_sem, device, sent=None, received=None):
        copy = Transfer(
            pltpu.make_async_remote_copy(
                src_ref=src, dst_ref=dst, send_sem=s_sem, recv_sem=r_sem, device_id=device, device_id_type=MESH
            ),
            sent,
            received,
        )
        sends.append(copy)
        return copy

    def send(*args, **kwargs):
        return plan(*args, **kwargs).start()

    y_b, y_pk, y_x, y_c, y_kv = [None], [None], [None], [None], [None]
    hand_b, hand_c = [None], [None]
    for k in range(1, NY):
        own_b, own_c = brow.at[y, core], crow.at[y, core]
        y_b.append(plan(own_b, own_b, y_s.at[0, k], y_r.at[0, k], y_peer[k]))
        y_pk.append(plan(pk.at[y_at[k]], prow.at[y], y_s.at[1, k], y_r.at[1, k], y_peer[k]))
        quarter = x_hbm.at[:, pl.ds(pl.multiple_of(y_at[k] * QW, QW), QW)]
        y_x.append(plan(quarter, xrow.at[y], y_s.at[2, k], y_r.at[2, k], y_peer[k]))
        y_c.append(plan(own_c, own_c, y_s.at[3, k], y_r.at[3, k], y_peer[k]))
        y_kv.append(plan(kv.at[core, 0, 0], kv.at[core, 0, NY - k], kvy_s.at[k], kvy_r.at[k], y_peer[k]))
        came_b, came_c = brow.at[y_at[NY - k], core], crow.at[y_at[NY - k], core]
        hand_b.append(plan(came_b, came_b, pair_s.at[3 + k], pair_r.at[3 + k], partner))
        hand_c.append(plan(came_c, came_c, pair_s.at[6 + k], pair_r.at[6 + k], partner))
    plus = {
        (s, k): plan(
            kv.at[core, s, k], kv.at[core, s + 1, k], kvp_s.at[s, k], kvp_r.at[s, k], next_row,
            (z >= s) & (z < NZ - 1), z >= s + 1,
        )
        for s in range(4)
        for k in range(NY)
    }
    far = {
        s: plan(
            kv.at[core, 0], kv.at[core, s], kvm_s.at[s - 5], kvm_r.at[s - 5], (lax.rem(z + s, NZ) * NY + y, head),
            z + s < NZ, z >= s,
        )
        for s in (5, 6, 7)
    }
    hand = []
    for slot in range(NZ):
        part = kv.at[core, slot, pl.ds(1, NY - 1)] if slot < 5 else kv.at[core, slot]
        used = None if slot == 0 else z >= slot
        hand.append(plan(part, part, kvh_s.at[slot], kvh_r.at[slot], partner, used, used))
    hand_own = [None]
    for slot in range(1, 5):
        part = kv.at[core, slot, 0]
        hand_own.append(plan(part, part, kvh_s.at[7 + slot], kvh_r.at[7 + slot], partner, z >= slot, z >= slot))
    z_chain = [
        plan(rz.at[i], rin.at[i], z_s.at[i], z_r.at[i], next_row, z < NZ - 1, z > 0) for i in range(NZ)
    ]
    y_out = [
        plan(gout.at[j], fs.at[y], y_s.at[4, j], y_r.at[4, y], (z * NY + j, head), y != j) for j in range(NY)
    ]
    y_in = [
        Transfer(
            pltpu.make_async_remote_copy(
                src_ref=gout.at[j], dst_ref=fs.at[j], send_sem=y_s.at[4, j], recv_sem=y_r.at[4, j],
                device_id=(z * NY + j, head), device_id_type=MESH,
            ),
            None,
            y != j,
        )
        for j in range(NY)
    ]
    swap = plan(sq_out, sq_in, pair_s.at[10], pair_r.at[10], partner)

    loads[0].wait()
    loads[1].wait()
    row = lax.broadcasted_iota(jnp.int32, (TOK, TOK), 0)
    col = lax.broadcasted_iota(jnp.int32, (TOK, TOK), 1)
    lower = col <= row
    lane = lax.broadcasted_iota(jnp.int32, (1, TOK), 1)
    left = lane < 64
    ld_t = ld_ref[...]
    cum = dot(lower.astype(F32), ld_t, NT, precision=HI)
    cum_t = dot(ld_t, (row <= col).astype(F32), precision=HI)
    dt_t = dt_ref[...]
    block_log = cum_t[:, TOK - 1 : TOK]
    weight_t = jnp.exp(block_log - cum_t) * dt_t
    log_t = jnp.broadcast_to(block_log, (HEADS, TOK))
    for quarter in range(NY):
        heads = slice(4 * quarter, 4 * quarter + 4)
        pk[quarter] = jnp.concatenate([weight_t[heads], log_t[heads]], axis=0)
    prow[y] = pk[y]
    for i in (2, 3, 4, 5):
        loads[i].wait()
    @pl.when(z == 0)
    def _():
        rin[...] = jnp.zeros_like(rin)

    pl.semaphore_wait(barrier, NY + jnp.where(z > 0, 1, 0) + jnp.where(z < NZ - 1, 1, 0) + jnp.maximum(z - 4, 0))

    for s in (5, 6, 7):

        @pl.when(z >= s)
        def _():
            pl.semaphore_signal(
                ready.at[s - 5], inc=1, device_id=(lax.rem(z + NZ - s, NZ) * NY + y, head), device_id_type=MESH
            )

    pair_k = send(khalf.at[core], khalf.at[core], pair_s.at[0], pair_r.at[0], partner)
    pair_v = send(vhalf.at[core], vhalf.at[core], pair_s.at[1], pair_r.at[1], partner)
    pair_b = send(brow.at[y, core], brow.at[y, core], pair_s.at[2], pair_r.at[2], partner)
    pair_c = send(crow.at[y, core], crow.at[y, core], pair_s.at[3], pair_r.at[3], partner)
    for k in range(1, NY):
        y_b[k].start()
        y_pk[k].start()
    for k in range(1, NY):
        y_x[k].start()

    pair_k.wait_recv()
    pair_v.wait_recv()
    kv[0, 0, 0] = khalf[...].reshape(128, TOK)
    kv[1, 0, 0] = vhalf[...].reshape(128, TOK).T

    def pump(s, blocks):
        for k in blocks:
            plus[s, k].wait_recv()
            if s < 3:
                plus[s + 1, k].start()

    plus[0, 0].start()

    loads[8].wait()

    for h in range(QH):
        stacked[h * TOK : (h + 1) * TOK] = q_ref[:, h * 128 : (h + 1) * 128]

    def attend(keys, values, first=False):
        for h in range(QH):
            rows = slice(h * TOK, (h + 1) * TOK)
            scores = [dot(stacked[rows], part) for part in keys]
            if first:
                scores = [jnp.where(lower, scores[0], NEGATIVE)]
            top = functools.reduce(jnp.maximum, scores)
            top = jnp.broadcast_to(jnp.max(top, axis=1, keepdims=True), (TOK, 128))
            if not first:
                before = m_ref[rows]
                top = jnp.maximum(before, top)
                factor = jnp.exp2((before - top) * SCALE)
            weights = [jnp.exp2((part - top) * SCALE) for part in scores]
            total = functools.reduce(jnp.add, weights)
            mixed = dot(jnp.concatenate([part.astype(BF) for part in weights], axis=1), values)
            m_ref[rows] = top
            l_ref[rows] = total if first else l_ref[rows] * factor + total
            acc_ref[rows] = mixed if first else acc_ref[rows] * factor + mixed

    late = z >= 5

    def attend_row(slot):
        hand[slot].wait_recv()

        @pl.when((z >= slot) & (~late if slot < 5 else late))
        def _():
            attend([kv[0, slot, k] for k in range(NY)], kv[1, slot].reshape(NY * TOK, 128))

        if slot < 5:

            @pl.when(late)
            def _():
                attend([kv[0, slot, k] for k in range(1, NY)], kv[1, slot, 1:].reshape((NY - 1) * TOK, 128))

    def attend_column():
        attend(
            [kv[0, slot, 0] for slot in range(1, 5)],
            jnp.concatenate([kv[1, slot, 0] for slot in range(1, 5)], axis=0),
        )

    attend([kv[0, 0, 0]], kv[1, 0, 0], first=True)
    pump(0, [0])
    hand_own[1].start()

    pair_b.wait_recv()
    pair_c.wait_recv()
    loads[6].wait()
    loads[9].wait()
    decay = jnp.exp(cum)
    inner = dot(crow[y, 0], brow[y, 0], NT) + dot(crow[y, 1], brow[y, 1], NT)
    for i in range(HEADS // 2):
        cols = slice(128 * i, 128 * (i + 1))
        x_two = x_ref[:, cols]
        parts = []
        for h in (2 * i, 2 * i + 1):
            gap = jnp.where(lower, cum[:, h : h + 1] - cum_t[h : h + 1, :], NEGATIVE)
            mix = (inner * jnp.exp(gap) * dt_t[h : h + 1, :]).astype(BF)
            parts.append(dot(mix, x_two))
        gain = jnp.where(left, skip_ref[:, 2 * i : 2 * i + 1], skip_ref[:, 2 * i + 1 : 2 * i + 2])
        gate = gate_ref[:, cols].astype(F32)
        gate = gate / (1.0 + jnp.exp(-gate))
        grow = jnp.where(left, decay[:, 2 * i : 2 * i + 1], decay[:, 2 * i + 1 : 2 * i + 2])
        yb[:, cols] = (jnp.where(left, parts[0], parts[1]) + gain * x_two.astype(F32)) * gate
        open_gate[:, cols] = gate * grow
        if i == 3:
            pump(1, [0])
            hand_own[2].start()
    pump(2, [0])
    hand_own[3].start()

    for k in range(1, NY):
        y_b[k].wait_recv()
        hand_b[k].start()
    loads[7].wait()
    for k in range(1, NY):
        y_pk[k].wait_recv()
        y_x[k].wait_recv()
    for k in range(1, NY):
        y_kv[k].start()
    for k in range(1, NY):
        y_c[k].start()
    for k in range(1, NY):
        hand_b[k].wait_recv()
    packed = prow[...]
    columns = packed.reshape(NY * 8, TOK).T

    def two_by_two(parts):
        return jnp.concatenate(
            [jnp.where(left, parts[0], parts[1]), jnp.where(left, parts[2], parts[3])], axis=1
        )

    logs = [two_by_two([packed[j, 4 + i : 5 + i] for i in range(4)]) for j in range(NY)]
    row_decay = jnp.exp(logs[0] + logs[1] + logs[2] + logs[3])
    state = None
    for j in range(NY):
        weight = two_by_two([columns[:, 8 * j + i : 8 * j + i + 1] for i in range(4)])
        weighted = (xrow[j].astype(F32) * weight).astype(BF)
        own = jnp.concatenate([dot(brow[j, 0], weighted, TN), dot(brow[j, 1], weighted, TN)], axis=0)
        state = own if state is None else state * jnp.exp(logs[j]) + own
        if j < NY - 1:
            prior[j + 1] = state.astype(BF)
    change[...] = state.reshape(NZ, 32, QW)
    pump(3, [0])
    hand_own[4].start()

    def share_row():
        for k in range(1, NY):
            y_kv[k].wait_recv()
            plus[0, NY - k].start()
        hand[0].start()

        for s in (5, 6, 7):

            @pl.when(z + s < NZ)
            def _():
                pl.semaphore_wait(ready.at[s - 5], 1)

            far[s].start()

    def row_part():
        for k in range(1, NY):
            y_c[k].wait_recv()
            hand_c[k].start()
        for k in range(1, NY):
            hand_c[k].wait_recv()
        for j in range(1, NY):
            early[j] = dot(crow[j, 0], prior[j, :128]) + dot(crow[j, 1], prior[j, 128:])

    def attend_own():
        hand[0].wait_recv()
        for k in range(1, NY):

            @pl.when(y + k >= NY)
            def _():
                attend([kv[0, 0, k]], kv[1, 0, k])


    @pl.when(z >= 4)
    def _():
        share_row()
        row_part()

    for copy in hand_own[1:]:
        copy.wait_recv()
    pl.when(late)(attend_column)
    pl.when(late)(attend_own)
    for i in range(NZ):
        z_chain[i].wait_recv()
        rz[i] = (rin[i].astype(F32) * row_decay + change[i]).astype(BF)
        z_chain[i].start()

    @pl.when(z < 4)
    def _():
        share_row()
        row_part()

    entering = rin[...].reshape(QW, QW)
    before = jnp.zeros((1, QW), F32)
    for j in range(NY):
        part = dot(crow[j, 0], entering[:128]) + dot(crow[j, 1], entering[128:])
        if j > 0:
            before = before + logs[j - 1]
            part = part * jnp.exp(before) + early[j]
        gout[j] = part.astype(BF)
        y_out[j].start()
    fs[y] = gout[y]

    pump(0, [1, 2, 3])
    hand[1].start()
    pl.when(~late)(attend_own)
    pump(1, [1, 2, 3])
    hand[2].start()
    attend_row(1)
    for slot in (7, 6, 5):
        far[slot].wait_recv()
        hand[slot].start()
    attend_row(2)
    attend_row(7)
    attend_row(6)
    pump(2, [1, 2, 3])
    hand[3].start()
    attend_row(5)
    pump(3, [1, 2, 3])
    hand[4].start()
    attend_row(3)
    attend_row(4)
    for h in range(QH):
        rows = slice(h * TOK, (h + 1) * TOK)
        attn_out[:, h * 128 : (h + 1) * 128] = (acc_ref[rows] / jnp.sum(l_ref[rows], axis=1, keepdims=True)).astype(BF)

    for copy in y_in:
        copy.wait_recv()
    squares = jnp.zeros((TOK, 128), F32)
    for i in range(HEADS // 2):
        cols = slice(128 * i, 128 * (i + 1))
        part = fs[i // 2, :, 128 * (i % 2) : 128 * (i % 2) + 128].astype(F32)
        gated = yb[:, cols] + open_gate[:, cols] * part
        yb[:, cols] = gated
        squares = squares + gated * gated
    own_sum = jnp.sum(squares, axis=1, keepdims=True)
    sq_out[...] = jnp.broadcast_to(own_sum, (TOK, 128))
    swap.start()
    swap.wait_recv()
    mean = (sq_out[...] + sq_in[...]) * (1.0 / 2048)
    scale = lax.rsqrt(mean + EPSILON)
    for i in range(HEADS // 2):
        cols = slice(128 * i, 128 * (i + 1))
        ssm_out[:, cols] = (yb[:, cols] * scale * gain_ref[:, cols]).astype(BF)
    for copy in sends:
        copy.wait_send()


def shards(
    ssm_input, ssm_gate, step_size, log_decay, input_b, input_c, skip_gain, norm_gain,
    attn_queries, attn_keys, attn_values,
):
    hbm = pl.BlockSpec(memory_space=pltpu.HBM)
    vmem = pl.BlockSpec(memory_space=pltpu.VMEM)
    dma = pltpu.SemaphoreType.DMA
    return pl.pallas_call(
        kernel,
        out_shape=(
            jax.ShapeDtypeStruct((TOK, 1024), BF),
            jax.ShapeDtypeStruct((TOK, 512), BF),
        ),
        in_specs=[hbm] * 6 + [vmem] * 2 + [hbm] * 3,
        out_specs=(vmem, vmem),
        scratch_shapes=[
            pltpu.VMEM((TOK, 1024), BF),
            pltpu.VMEM((TOK, 1024), BF),
            pltpu.VMEM((HEADS, TOK), F32),
            pltpu.VMEM((HEADS, TOK), F32),
            pltpu.VMEM((TOK, 512), BF),
            pltpu.VMEM((2, 64, TOK), BF),
            pltpu.VMEM((2, 64, TOK), BF),
            pltpu.VMEM((NY, 2, TOK, 128), BF),
            pltpu.VMEM((NY, 2, TOK, 128), BF),
            pltpu.VMEM((NY, TOK, QW), BF),
            pltpu.VMEM((NY, 8, TOK), F32),
            pltpu.VMEM((NY, 8, TOK), F32),
            pltpu.VMEM((NZ, 32, QW), F32),
            pltpu.VMEM((NY, QW, QW), BF),
            pltpu.VMEM((NZ, 32, QW), BF),
            pltpu.VMEM((NZ, 32, QW), BF),
            pltpu.VMEM((NY, TOK, QW), F32),
            pltpu.VMEM((NY, TOK, QW), BF),
            pltpu.VMEM((NY, TOK, QW), BF),
            pltpu.VMEM((2, NZ, NY, TOK, 128), BF),
            pltpu.VMEM((QH * TOK, 128), F32),
            pltpu.VMEM((QH * TOK, 128), F32),
            pltpu.VMEM((QH * TOK, 128), F32),
            pltpu.VMEM((QH * TOK, 128), BF),
            pltpu.VMEM((TOK, 1024), F32),
            pltpu.VMEM((TOK, 1024), F32),
            pltpu.VMEM((TOK, 128), F32),
            pltpu.VMEM((TOK, 128), F32),
            dma((10,)),
            dma((11,)),
            dma((11,)),
            dma((5, NY)),
            dma((5, NY)),
            dma((NZ,)),
            dma((NZ,)),
            dma((NY,)),
            dma((NY,)),
            dma((4, NY)),
            dma((4, NY)),
            dma((3,)),
            dma((3,)),
            dma((12,)),
            dma((12,)),
            pltpu.SemaphoreType.REGULAR((3,)),
        ],
        name="hybrid_mixer",
        compiler_params=pltpu.CompilerParams(
            collective_id=0, has_side_effects=True, vmem_limit_bytes=56 << 20
        ),
    )(
        ssm_input, ssm_gate, step_size.T, log_decay.T, input_b, input_c,
        skip_gain.reshape(1, HEADS), norm_gain.reshape(1, 1024),
        attn_queries, attn_keys.T, attn_values.T,
    )


def solution(mesh):
    split = P("ctx", "head")
    return jax.shard_map(
        shards,
        mesh=mesh,
        in_specs=(split,) * 6 + (P("head"), P("head")) + (split,) * 3,
        out_specs=(split, split),
        check_vma=False,
    )
```

```python
import functools
import math

import jax
import jax.numpy as jnp
from jax import lax
from jax.experimental import pallas as pl
from jax.experimental.pallas import tpu as pltpu
from jax.sharding import PartitionSpec as P

MESH = pl.DeviceIdType.MESH
BF = jnp.bfloat16
F32 = jnp.float32
HI = lax.Precision.HIGHEST

TOK = 128
NZ, NY = 8, 4
HEADS = 16
QW = 256
QH = 4
EPSILON = 1e-05
NEGATIVE = -1e30
SCALE = math.log2(math.e) / math.sqrt(128)

NT = (((1,), (1,)), ((), ()))
TN = (((0,), (0,)), ((), ()))


def dot(a, b, dims=(((1,), (0,)), ((), ())), precision=None):
    return lax.dot_general(a, b, dims, precision=precision, preferred_element_type=F32)


class Transfer:
    def __init__(self, copy, sent=None, received=None):
        self.copy, self.sent, self.received = copy, sent, received

    @staticmethod
    def under(condition, action):
        if condition is None:
            action()
        else:
            pl.when(condition)(lambda: action())

    def start(self):
        self.under(self.sent, self.copy.start)
        return self

    def wait_recv(self):
        self.under(self.received, self.copy.wait_recv)

    def wait_send(self):
        self.under(self.sent, self.copy.wait_send)


def kernel(
    x_hbm, gate_hbm, dt_hbm, ld_hbm, b_hbm, c_hbm, skip_ref, gain_ref, q_hbm, k_hbm, v_hbm,
    ssm_out, attn_out,
    x_ref, gate_ref, dt_ref, ld_ref, q_ref, khalf, vhalf,
    brow, crow, xrow, pk, prow, change, prior, rz, rin, early, gout, fs,
    kv, m_ref, l_ref, acc_ref, stacked, yb, open_gate, sq_out, sq_in,
    load_sem, pair_s, pair_r, y_s, y_r, z_s, z_r, kvy_s, kvy_r, kvp_s, kvp_r, kvm_s, kvm_r, kvh_s, kvh_r, ready,
):
    ctx = lax.axis_index("ctx")
    head = lax.axis_index("head")
    z, y = lax.div(ctx, NY), lax.rem(ctx, NY)
    core = lax.rem(head, 2)
    partner = (ctx, head + 1 - 2 * core)
    y_peer = [None] + [(z * NY + lax.rem(y + k, NY), head) for k in range(1, NY)]
    next_row = (lax.rem(z + 1, NZ) * NY + y, head)
    last_row = (lax.rem(z + NZ - 1, NZ) * NY + y, head)
    y_at = [lax.rem(y + k, NY) for k in range(NY)]

    barrier = pltpu.get_barrier_semaphore()

    def greet(peer):
        pl.semaphore_signal(barrier, inc=1, device_id=peer, device_id_type=MESH)

    for peer in [partner] + y_peer[1:]:
        greet(peer)
    pl.when(z > 0)(lambda: greet(last_row))
    pl.when(z < NZ - 1)(lambda: greet(next_row))
    for s in (5, 6, 7):

        @pl.when(z + s < NZ)
        def _():
            greet((lax.rem(z + s, NZ) * NY + y, head))


    loads = [
        pltpu.make_async_copy(src, dst, load_sem.at[i])
        for i, (src, dst) in enumerate(
            [
                (dt_hbm, dt_ref),
                (ld_hbm, ld_ref),
                (k_hbm, khalf.at[core]),
                (v_hbm, vhalf.at[core]),
                (b_hbm, brow.at[y, core]),
                (c_hbm, crow.at[y, core]),
                (x_hbm, x_ref),
                (x_hbm.at[:, pl.ds(pl.multiple_of(y * QW, QW), QW)], xrow.at[y]),
                (q_hbm, q_ref),
                (gate_hbm, gate_ref),
            ]
        )
    ]
    for load in loads:
        load.start()

    sends = []

    def plan(src, dst, s_sem, r_sem, device, sent=None, received=None):
        copy = Transfer(
            pltpu.make_async_remote_copy(
                src_ref=src, dst_ref=dst, send_sem=s_sem, recv_sem=r_sem, device_id=device, device_id_type=MESH
            ),
            sent,
            received,
        )
        sends.append(copy)
        return copy

    def send(*args, **kwargs):
        return plan(*args, **kwargs).start()

    y_b, y_pk, y_x, y_c, y_kv = [None], [None], [None], [None], [None]
    hand_b, hand_c = [None], [None]
    for k in range(1, NY):
        own_b, own_c = brow.at[y, core], crow.at[y, core]
        y_b.append(plan(own_b, own_b, y_s.at[0, k], y_r.at[0, k], y_peer[k]))
        y_pk.append(plan(pk.at[y_at[k]], prow.at[y], y_s.at[1, k], y_r.at[1, k], y_peer[k]))
        quarter = x_hbm.at[:, pl.ds(pl.multiple_of(y_at[k] * QW, QW), QW)]
        y_x.append(plan(quarter, xrow.at[y], y_s.at[2, k], y_r.at[2, k], y_peer[k]))
        y_c.append(plan(own_c, own_c, y_s.at[3, k], y_r.at[3, k], y_peer[k]))
        y_kv.append(plan(kv.at[core, 0, 0], kv.at[core, 0, NY - k], kvy_s.at[k], kvy_r.at[k], y_peer[k]))
        came_b, came_c = brow.at[y_at[NY - k], core], crow.at[y_at[NY - k], core]
        hand_b.append(plan(came_b, came_b, pair_s.at[3 + k], pair_r.at[3 + k], partner))
        hand_c.append(plan(came_c, came_c, pair_s.at[6 + k], pair_r.at[6 + k], partner))
    plus = {
        (s, k): plan(
            kv.at[core, s, k], kv.at[core, s + 1, k], kvp_s.at[s, k], kvp_r.at[s, k], next_row,
            (z >= s) & (z < NZ - 1), z >= s + 1,
        )
        for s in range(4)
        for k in range(NY)
    }
    far = {
        s: plan(
            kv.at[core, 0], kv.at[core, s], kvm_s.at[s - 5], kvm_r.at[s - 5], (lax.rem(z + s, NZ) * NY + y, head),
            z + s < NZ, z >= s,
        )
        for s in (5, 6, 7)
    }
    hand = []
    for slot in range(NZ):
        part = kv.at[core, slot, pl.ds(1, NY - 1)] if slot < 5 else kv.at[core, slot]
        used = None if slot == 0 else z >= slot
        hand.append(plan(part, part, kvh_s.at[slot], kvh_r.at[slot], partner, used, used))
    hand_own = [None]
    for slot in range(1, 5):
        part = kv.at[core, slot, 0]
        hand_own.append(plan(part, part, kvh_s.at[7 + slot], kvh_r.at[7 + slot], partner, z >= slot, z >= slot))
    z_chain = [
        plan(rz.at[i], rin.at[i], z_s.at[i], z_r.at[i], next_row, z < NZ - 1, z > 0) for i in range(NZ)
    ]
    y_out = [
        plan(gout.at[j], fs.at[y], y_s.at[4, j], y_r.at[4, y], (z * NY + j, head), y != j) for j in range(NY)
    ]
    y_in = [
        Transfer(
            pltpu.make_async_remote_copy(
                src_ref=gout.at[j], dst_ref=fs.at[j], send_sem=y_s.at[4, j], recv_sem=y_r.at[4, j],
                device_id=(z * NY + j, head), device_id_type=MESH,
            ),
            None,
            y != j,
        )
        for j in range(NY)
    ]
    swap = plan(sq_out, sq_in, pair_s.at[10], pair_r.at[10], partner)

    loads[0].wait()
    loads[1].wait()
    row = lax.broadcasted_iota(jnp.int32, (TOK, TOK), 0)
    col = lax.broadcasted_iota(jnp.int32, (TOK, TOK), 1)
    lower = col <= row
    lane = lax.broadcasted_iota(jnp.int32, (1, TOK), 1)
    left = lane < 64
    ld_t = ld_ref[...]
    cum = dot(lower.astype(F32), ld_t, NT, precision=HI)
    cum_t = dot(ld_t, (row <= col).astype(F32), precision=HI)
    dt_t = dt_ref[...]
    block_log = cum_t[:, TOK - 1 : TOK]
    weight_t = jnp.exp(block_log - cum_t) * dt_t
    log_t = jnp.broadcast_to(block_log, (HEADS, TOK))
    for quarter in range(NY):
        heads = slice(4 * quarter, 4 * quarter + 4)
        pk[quarter] = jnp.concatenate([weight_t[heads], log_t[heads]], axis=0)
    prow[y] = pk[y]
    for i in (2, 3, 4, 5):
        loads[i].wait()
    @pl.when(z == 0)
    def _():
        rin[...] = jnp.zeros_like(rin)

    pl.semaphore_wait(barrier, NY + jnp.where(z > 0, 1, 0) + jnp.where(z < NZ - 1, 1, 0) + jnp.maximum(z - 4, 0))

    for s in (5, 6, 7):

        @pl.when(z >= s)
        def _():
            pl.semaphore_signal(
                ready.at[s - 5], inc=1, device_id=(lax.rem(z + NZ - s, NZ) * NY + y, head), device_id_type=MESH
            )

    pair_k = send(khalf.at[core], khalf.at[core], pair_s.at[0], pair_r.at[0], partner)
    pair_v = send(vhalf.at[core], vhalf.at[core], pair_s.at[1], pair_r.at[1], partner)
    pair_b = send(brow.at[y, core], brow.at[y, core], pair_s.at[2], pair_r.at[2], partner)
    pair_c = send(crow.at[y, core], crow.at[y, core], pair_s.at[3], pair_r.at[3], partner)
    for k in range(1, NY):
        y_b[k].start()
        y_pk[k].start()
    for k in range(1, NY):
        y_x[k].start()

    pair_k.wait_recv()
    pair_v.wait_recv()
    kv[0, 0, 0] = khalf[...].reshape(128, TOK)
    kv[1, 0, 0] = vhalf[...].reshape(128, TOK).T

    def pump(s, blocks):
        for k in blocks:
            plus[s, k].wait_recv()
            if s < 3:
                plus[s + 1, k].start()

    plus[0, 0].start()

    loads[8].wait()

    for h in range(QH):
        stacked[h * TOK : (h + 1) * TOK] = q_ref[:, h * 128 : (h + 1) * 128]

    def attend(keys, values, first=False):
        for h in range(QH):
            rows = slice(h * TOK, (h + 1) * TOK)
            scores = [dot(stacked[rows], part) for part in keys]
            if first:
                scores = [jnp.where(lower, scores[0], NEGATIVE)]
            top = functools.reduce(jnp.maximum, scores)
            top = jnp.broadcast_to(jnp.max(top, axis=1, keepdims=True), (TOK, 128))
            if not first:
                before = m_ref[rows]
                top = jnp.maximum(before, top)
                factor = jnp.exp2((before - top) * SCALE)
            weights = [jnp.exp2((part - top) * SCALE) for part in scores]
            total = functools.reduce(jnp.add, weights)
            mixed = dot(jnp.concatenate([part.astype(BF) for part in weights], axis=1), values)
            m_ref[rows] = top
            l_ref[rows] = total if first else l_ref[rows] * factor + total
            acc_ref[rows] = mixed if first else acc_ref[rows] * factor + mixed

    late = z >= 5

    def attend_row(slot):
        hand[slot].wait_recv()

        @pl.when((z >= slot) & (~late if slot < 5 else late))
        def _():
            attend([kv[0, slot, k] for k in range(NY)], kv[1, slot].reshape(NY * TOK, 128))

        if slot < 5:

            @pl.when(late)
            def _():
                attend([kv[0, slot, k] for k in range(1, NY)], kv[1, slot, 1:].reshape((NY - 1) * TOK, 128))

    def attend_column():
        attend(
            [kv[0, slot, 0] for slot in range(1, 5)],
            jnp.concatenate([kv[1, slot, 0] for slot in range(1, 5)], axis=0),
        )

    attend([kv[0, 0, 0]], kv[1, 0, 0], first=True)
    pump(0, [0])
    hand_own[1].start()

    pair_b.wait_recv()
    pair_c.wait_recv()
    loads[6].wait()
    loads[9].wait()
    decay = jnp.exp(cum)
    inner = dot(crow[y, 0], brow[y, 0], NT) + dot(crow[y, 1], brow[y, 1], NT)
    for i in range(HEADS // 2):
        cols = slice(128 * i, 128 * (i + 1))
        x_two = x_ref[:, cols]
        parts = []
        for h in (2 * i, 2 * i + 1):
            gap = jnp.where(lower, cum[:, h : h + 1] - cum_t[h : h + 1, :], NEGATIVE)
            mix = (inner * jnp.exp(gap) * dt_t[h : h + 1, :]).astype(BF)
            parts.append(dot(mix, x_two))
        gain = jnp.where(left, skip_ref[:, 2 * i : 2 * i + 1], skip_ref[:, 2 * i + 1 : 2 * i + 2])
        gate = gate_ref[:, cols].astype(F32)
        gate = gate / (1.0 + jnp.exp(-gate))
        grow = jnp.where(left, decay[:, 2 * i : 2 * i + 1], decay[:, 2 * i + 1 : 2 * i + 2])
        yb[:, cols] = (jnp.where(left, parts[0], parts[1]) + gain * x_two.astype(F32)) * gate
        open_gate[:, cols] = gate * grow
        if i == 3:
            pump(1, [0])
            hand_own[2].start()
    pump(2, [0])
    hand_own[3].start()

    for k in range(1, NY):
        y_b[k].wait_recv()
        hand_b[k].start()
    loads[7].wait()
    for k in range(1, NY):
        y_pk[k].wait_recv()
        y_x[k].wait_recv()
    for k in range(1, NY):
        y_kv[k].start()
    for k in range(1, NY):
        y_c[k].start()
    for k in range(1, NY):
        hand_b[k].wait_recv()
    packed = prow[...]
    columns = packed.reshape(NY * 8, TOK).T

    def two_by_two(parts):
        return jnp.concatenate(
            [jnp.where(left, parts[0], parts[1]), jnp.where(left, parts[2], parts[3])], axis=1
        )

    logs = [two_by_two([packed[j, 4 + i : 5 + i] for i in range(4)]) for j in range(NY)]
    row_decay = jnp.exp(logs[0] + logs[1] + logs[2] + logs[3])
    state = None
    for j in range(NY):
        weight = two_by_two([columns[:, 8 * j + i : 8 * j + i + 1] for i in range(4)])
        weighted = (xrow[j].astype(F32) * weight).astype(BF)
        own = jnp.concatenate([dot(brow[j, 0], weighted, TN), dot(brow[j, 1], weighted, TN)], axis=0)
        state = own if state is None else state * jnp.exp(logs[j]) + own
        if j < NY - 1:
            prior[j + 1] = state.astype(BF)
    change[...] = state.reshape(NZ, 32, QW)
    pump(3, [0])
    hand_own[4].start()

    def share_row():
        for k in range(1, NY):
            y_kv[k].wait_recv()
            plus[0, NY - k].start()
        hand[0].start()

        for s in (5, 6, 7):

            @pl.when(z + s < NZ)
            def _():
                pl.semaphore_wait(ready.at[s - 5], 1)

            far[s].start()

    def row_part():
        for k in range(1, NY):
            y_c[k].wait_recv()
            hand_c[k].start()
        for k in range(1, NY):
            hand_c[k].wait_recv()
        for j in range(1, NY):
            early[j] = dot(crow[j, 0], prior[j, :128]) + dot(crow[j, 1], prior[j, 128:])

    def attend_own():
        hand[0].wait_recv()
        for k in range(1, NY):

            @pl.when(y + k >= NY)
            def _():
                attend([kv[0, 0, k]], kv[1, 0, k])


    @pl.when(z >= 4)
    def _():
        share_row()
        row_part()

    for copy in hand_own[1:]:
        copy.wait_recv()
    pl.when(late)(attend_column)
    pl.when(late)(attend_own)
    for i in range(NZ):
        z_chain[i].wait_recv()
        rz[i] = (rin[i].astype(F32) * row_decay + change[i]).astype(BF)
        z_chain[i].start()

    @pl.when(z < 4)
    def _():
        share_row()
        row_part()

    entering = rin[...].reshape(QW, QW)
    before = jnp.zeros((1, QW), F32)
    for j in range(NY):
        part = dot(crow[j, 0], entering[:128]) + dot(crow[j, 1], entering[128:])
        if j > 0:
            before = before + logs[j - 1]
            part = part * jnp.exp(before) + early[j]
        gout[j] = part.astype(BF)
        y_out[j].start()
    fs[y] = gout[y]

    pump(0, [1, 2, 3])
    hand[1].start()
    pl.when(~late)(attend_own)
    pump(1, [1, 2, 3])
    hand[2].start()
    attend_row(1)
    for slot in (7, 6, 5):
        far[slot].wait_recv()
        hand[slot].start()
    attend_row(2)
    attend_row(7)
    attend_row(6)
    pump(2, [1, 2, 3])
    hand[3].start()
    attend_row(5)
    pump(3, [1, 2, 3])
    hand[4].start()
    attend_row(3)
    attend_row(4)
    for h in range(QH):
        rows = slice(h * TOK, (h + 1) * TOK)
        attn_out[:, h * 128 : (h + 1) * 128] = (acc_ref[rows] / jnp.sum(l_ref[rows], axis=1, keepdims=True)).astype(BF)

    for copy in y_in:
        copy.wait_recv()
    squares = jnp.zeros((TOK, 128), F32)
    for i in range(HEADS // 2):
        cols = slice(128 * i, 128 * (i + 1))
        part = fs[i // 2, :, 128 * (i % 2) : 128 * (i % 2) + 128].astype(F32)
        gated = yb[:, cols] + open_gate[:, cols] * part
        yb[:, cols] = gated
        squares = squares + gated * gated
    own_sum = jnp.sum(squares, axis=1, keepdims=True)
    sq_out[...] = jnp.broadcast_to(own_sum, (TOK, 128))
    swap.start()
    swap.wait_recv()
    mean = (sq_out[...] + sq_in[...]) * (1.0 / 2048)
    scale = lax.rsqrt(mean + EPSILON)
    for i in range(HEADS // 2):
        cols = slice(128 * i, 128 * (i + 1))
        ssm_out[:, cols] = (yb[:, cols] * scale * gain_ref[:, cols]).astype(BF)
    for copy in sends:
        copy.wait_send()


def hand_out(ssm, attention, ssm_out, attn_out):
    ssm_out[...] = ssm[...]
    attn_out[...] = attention[...]


def shards(
    ssm_input, ssm_gate, step_size, log_decay, input_b, input_c, skip_gain, norm_gain,
    attn_queries, attn_keys, attn_values,
):
    hbm = pl.BlockSpec(memory_space=pltpu.HBM)
    vmem = pl.BlockSpec(memory_space=pltpu.VMEM)
    dma = pltpu.SemaphoreType.DMA
    ssm, attention = pl.pallas_call(
        kernel,
        out_shape=(
            jax.ShapeDtypeStruct((TOK, 1024), BF),
            jax.ShapeDtypeStruct((TOK, 512), BF),
        ),
        in_specs=[hbm] * 6 + [vmem] * 2 + [hbm] * 3,
        out_specs=(vmem, vmem),
        scratch_shapes=[
            pltpu.VMEM((TOK, 1024), BF),
            pltpu.VMEM((TOK, 1024), BF),
            pltpu.VMEM((HEADS, TOK), F32),
            pltpu.VMEM((HEADS, TOK), F32),
            pltpu.VMEM((TOK, 512), BF),
            pltpu.VMEM((2, 64, TOK), BF),
            pltpu.VMEM((2, 64, TOK), BF),
            pltpu.VMEM((NY, 2, TOK, 128), BF),
            pltpu.VMEM((NY, 2, TOK, 128), BF),
            pltpu.VMEM((NY, TOK, QW), BF),
            pltpu.VMEM((NY, 8, TOK), F32),
            pltpu.VMEM((NY, 8, TOK), F32),
            pltpu.VMEM((NZ, 32, QW), F32),
            pltpu.VMEM((NY, QW, QW), BF),
            pltpu.VMEM((NZ, 32, QW), BF),
            pltpu.VMEM((NZ, 32, QW), BF),
            pltpu.VMEM((NY, TOK, QW), F32),
            pltpu.VMEM((NY, TOK, QW), BF),
            pltpu.VMEM((NY, TOK, QW), BF),
            pltpu.VMEM((2, NZ, NY, TOK, 128), BF),
            pltpu.VMEM((QH * TOK, 128), F32),
            pltpu.VMEM((QH * TOK, 128), F32),
            pltpu.VMEM((QH * TOK, 128), F32),
            pltpu.VMEM((QH * TOK, 128), BF),
            pltpu.VMEM((TOK, 1024), F32),
            pltpu.VMEM((TOK, 1024), F32),
            pltpu.VMEM((TOK, 128), F32),
            pltpu.VMEM((TOK, 128), F32),
            dma((10,)),
            dma((11,)),
            dma((11,)),
            dma((5, NY)),
            dma((5, NY)),
            dma((NZ,)),
            dma((NZ,)),
            dma((NY,)),
            dma((NY,)),
            dma((4, NY)),
            dma((4, NY)),
            dma((3,)),
            dma((3,)),
            dma((12,)),
            dma((12,)),
            pltpu.SemaphoreType.REGULAR((3,)),
        ],
        name="hybrid_mixer",
        compiler_params=pltpu.CompilerParams(
            collective_id=0, has_side_effects=True, vmem_limit_bytes=56 << 20
        ),
    )(
        ssm_input, ssm_gate, step_size.T, log_decay.T, input_b, input_c,
        skip_gain.reshape(1, HEADS), norm_gain.reshape(1, 1024),
        attn_queries, attn_keys.T, attn_values.T,
    )
    return pl.pallas_call(
        hand_out,
        out_shape=(
            jax.ShapeDtypeStruct((TOK, 1024), BF),
            jax.ShapeDtypeStruct((TOK, 512), BF),
        ),
        in_specs=[vmem] * 2,
        out_specs=(vmem, vmem),
        name="hand_out",
    )(ssm, attention)


def solution(mesh):
    split = P("ctx", "head")
    return jax.shard_map(
        shards,
        mesh=mesh,
        in_specs=(split,) * 6 + (P("head"), P("head")) + (split,) * 3,
        out_specs=(split, split),
        check_vma=False,
    )
```

```python
import functools
import math

import jax
import jax.numpy as jnp
from jax import lax
from jax.experimental import pallas as pl
from jax.experimental.pallas import tpu as pltpu
from jax.sharding import PartitionSpec as P

MESH = pl.DeviceIdType.MESH
BF = jnp.bfloat16
F32 = jnp.float32
HI = lax.Precision.HIGHEST

TOK = 128
PIECES = 16
NZ, NY = 8, 4
HEADS = 16
QW = 256
QH = 4
EPSILON = 1e-05
NEGATIVE = -1e30
SCALE = math.log2(math.e) / math.sqrt(128)

NT = (((1,), (1,)), ((), ()))
TN = (((0,), (0,)), ((), ()))


def dot(a, b, dims=(((1,), (0,)), ((), ())), precision=None):
    return lax.dot_general(a, b, dims, precision=precision, preferred_element_type=F32)


class Transfer:
    def __init__(self, copy, sent=None, received=None):
        self.copy, self.sent, self.received = copy, sent, received

    @staticmethod
    def under(condition, action):
        if condition is None:
            action()
        else:
            pl.when(condition)(lambda: action())

    def start(self):
        self.under(self.sent, self.copy.start)
        return self

    def wait_recv(self):
        self.under(self.received, self.copy.wait_recv)

    def wait_send(self):
        self.under(self.sent, self.copy.wait_send)


def kernel(
    x_hbm, gate_hbm, dt_hbm, ld_hbm, b_hbm, c_hbm, skip_ref, gain_ref, q_hbm, k_hbm, v_hbm,
    ssm_out, attn_out,
    x_ref, gate_ref, dt_ref, ld_ref, q_ref, khalf, vhalf,
    brow, crow, xrow, pk, prow, change, prior, rz, rin, early, gout, fs,
    kv, m_ref, l_ref, acc_ref, stacked, yb, open_gate, sq_out, sq_in,
    load_sem, pair_s, pair_r, y_s, y_r, z_s, z_r, kvy_s, kvy_r, kvp_s, kvp_r, kvm_s, kvm_r, kvh_s, kvh_r, ready,
):
    ctx = lax.axis_index("ctx")
    head = lax.axis_index("head")
    z, y = lax.div(ctx, NY), lax.rem(ctx, NY)
    core = lax.rem(head, 2)
    partner = (ctx, head + 1 - 2 * core)
    y_peer = [None] + [(z * NY + lax.rem(y + k, NY), head) for k in range(1, NY)]
    next_row = (lax.rem(z + 1, NZ) * NY + y, head)
    last_row = (lax.rem(z + NZ - 1, NZ) * NY + y, head)
    y_at = [lax.rem(y + k, NY) for k in range(NY)]

    barrier = pltpu.get_barrier_semaphore()

    def greet(peer):
        pl.semaphore_signal(barrier, inc=1, device_id=peer, device_id_type=MESH)

    for peer in [partner] + y_peer[1:]:
        greet(peer)
    pl.when(z > 0)(lambda: greet(last_row))
    pl.when(z < NZ - 1)(lambda: greet(next_row))
    for s in (5, 6, 7):

        @pl.when(z + s < NZ)
        def _():
            greet((lax.rem(z + s, NZ) * NY + y, head))


    loads = [
        pltpu.make_async_copy(src, dst, load_sem.at[i])
        for i, (src, dst) in enumerate(
            [
                (dt_hbm, dt_ref),
                (ld_hbm, ld_ref),
                (k_hbm, khalf.at[core]),
                (v_hbm, vhalf.at[core]),
                (b_hbm, brow.at[y, core]),
                (c_hbm, crow.at[y, core]),
                (x_hbm, x_ref),
                (x_hbm.at[:, pl.ds(pl.multiple_of(y * QW, QW), QW)], xrow.at[y]),
                (q_hbm, q_ref),
                (gate_hbm, gate_ref),
            ]
        )
    ]
    for load in loads:
        load.start()

    sends = []

    def plan(src, dst, s_sem, r_sem, device, sent=None, received=None):
        copy = Transfer(
            pltpu.make_async_remote_copy(
                src_ref=src, dst_ref=dst, send_sem=s_sem, recv_sem=r_sem, device_id=device, device_id_type=MESH
            ),
            sent,
            received,
        )
        sends.append(copy)
        return copy

    def send(*args, **kwargs):
        return plan(*args, **kwargs).start()

    y_b, y_pk, y_x, y_c, y_kv = [None], [None], [None], [None], [None]
    hand_b, hand_c = [None], [None]
    for k in range(1, NY):
        own_b, own_c = brow.at[y, core], crow.at[y, core]
        y_b.append(plan(own_b, own_b, y_s.at[0, k], y_r.at[0, k], y_peer[k]))
        y_pk.append(plan(pk.at[y_at[k]], prow.at[y], y_s.at[1, k], y_r.at[1, k], y_peer[k]))
        quarter = x_hbm.at[:, pl.ds(pl.multiple_of(y_at[k] * QW, QW), QW)]
        y_x.append(plan(quarter, xrow.at[y], y_s.at[2, k], y_r.at[2, k], y_peer[k]))
        y_c.append(plan(own_c, own_c, y_s.at[3, k], y_r.at[3, k], y_peer[k]))
        y_kv.append(plan(kv.at[core, 0, 0], kv.at[core, 0, NY - k], kvy_s.at[k], kvy_r.at[k], y_peer[k]))
        came_b, came_c = brow.at[y_at[NY - k], core], crow.at[y_at[NY - k], core]
        hand_b.append(plan(came_b, came_b, pair_s.at[3 + k], pair_r.at[3 + k], partner))
        hand_c.append(plan(came_c, came_c, pair_s.at[6 + k], pair_r.at[6 + k], partner))
    plus = {
        (s, k): plan(
            kv.at[core, s, k], kv.at[core, s + 1, k], kvp_s.at[s, k], kvp_r.at[s, k], next_row,
            (z >= s) & (z < NZ - 1), z >= s + 1,
        )
        for s in range(4)
        for k in range(NY)
    }
    far = {
        s: plan(
            kv.at[core, 0], kv.at[core, s], kvm_s.at[s - 5], kvm_r.at[s - 5], (lax.rem(z + s, NZ) * NY + y, head),
            z + s < NZ, z >= s,
        )
        for s in (5, 6, 7)
    }
    hand = []
    for slot in range(NZ):
        part = kv.at[core, slot, pl.ds(1, NY - 1)] if slot < 5 else kv.at[core, slot]
        used = None if slot == 0 else z >= slot
        hand.append(plan(part, part, kvh_s.at[slot], kvh_r.at[slot], partner, used, used))
    hand_own = [None]
    for slot in range(1, 5):
        part = kv.at[core, slot, 0]
        hand_own.append(plan(part, part, kvh_s.at[7 + slot], kvh_r.at[7 + slot], partner, z >= slot, z >= slot))
    z_chain = [
        plan(rz.at[i], rin.at[i], z_s.at[i], z_r.at[i], next_row, z < NZ - 1, z > 0) for i in range(PIECES)
    ]
    y_out = [
        plan(gout.at[j], fs.at[y], y_s.at[4, j], y_r.at[4, y], (z * NY + j, head), y != j) for j in range(NY)
    ]
    y_in = [
        Transfer(
            pltpu.make_async_remote_copy(
                src_ref=gout.at[j], dst_ref=fs.at[j], send_sem=y_s.at[4, j], recv_sem=y_r.at[4, j],
                device_id=(z * NY + j, head), device_id_type=MESH,
            ),
            None,
            y != j,
        )
        for j in range(NY)
    ]
    swap = plan(sq_out, sq_in, pair_s.at[10], pair_r.at[10], partner)

    loads[0].wait()
    loads[1].wait()
    row = lax.broadcasted_iota(jnp.int32, (TOK, TOK), 0)
    col = lax.broadcasted_iota(jnp.int32, (TOK, TOK), 1)
    lower = col <= row
    lane = lax.broadcasted_iota(jnp.int32, (1, TOK), 1)
    left = lane < 64
    ld_t = ld_ref[...]
    cum = dot(lower.astype(F32), ld_t, NT, precision=HI)
    cum_t = dot(ld_t, (row <= col).astype(F32), precision=HI)
    dt_t = dt_ref[...]
    block_log = cum_t[:, TOK - 1 : TOK]
    weight_t = jnp.exp(block_log - cum_t) * dt_t
    log_t = jnp.broadcast_to(block_log, (HEADS, TOK))
    for quarter in range(NY):
        heads = slice(4 * quarter, 4 * quarter + 4)
        pk[quarter] = jnp.concatenate([weight_t[heads], log_t[heads]], axis=0)
    prow[y] = pk[y]
    for i in (2, 3, 4, 5):
        loads[i].wait()
    @pl.when(z == 0)
    def _():
        rin[...] = jnp.zeros_like(rin)

    pl.semaphore_wait(barrier, NY + jnp.where(z > 0, 1, 0) + jnp.where(z < NZ - 1, 1, 0) + jnp.maximum(z - 4, 0))

    for s in (5, 6, 7):

        @pl.when(z >= s)
        def _():
            pl.semaphore_signal(
                ready.at[s - 5], inc=1, device_id=(lax.rem(z + NZ - s, NZ) * NY + y, head), device_id_type=MESH
            )

    pair_k = send(khalf.at[core], khalf.at[core], pair_s.at[0], pair_r.at[0], partner)
    pair_v = send(vhalf.at[core], vhalf.at[core], pair_s.at[1], pair_r.at[1], partner)
    pair_b = send(brow.at[y, core], brow.at[y, core], pair_s.at[2], pair_r.at[2], partner)
    pair_c = send(crow.at[y, core], crow.at[y, core], pair_s.at[3], pair_r.at[3], partner)
    for k in range(1, NY):
        y_b[k].start()
        y_pk[k].start()
    for k in range(1, NY):
        y_x[k].start()

    pair_k.wait_recv()
    pair_v.wait_recv()
    kv[0, 0, 0] = khalf[...].reshape(128, TOK)
    kv[1, 0, 0] = vhalf[...].reshape(128, TOK).T

    def pump(s, blocks):
        for k in blocks:
            plus[s, k].wait_recv()
            if s < 3:
                plus[s + 1, k].start()

    plus[0, 0].start()

    loads[8].wait()

    for h in range(QH):
        stacked[h * TOK : (h + 1) * TOK] = q_ref[:, h * 128 : (h + 1) * 128]

    def attend(keys, values, first=False):
        for h in range(QH):
            rows = slice(h * TOK, (h + 1) * TOK)
            scores = [dot(stacked[rows], part) for part in keys]
            if first:
                scores = [jnp.where(lower, scores[0], NEGATIVE)]
            top = functools.reduce(jnp.maximum, scores)
            top = jnp.broadcast_to(jnp.max(top, axis=1, keepdims=True), (TOK, 128))
            if not first:
                before = m_ref[rows]
                top = jnp.maximum(before, top)
                factor = jnp.exp2((before - top) * SCALE)
            weights = [jnp.exp2((part - top) * SCALE) for part in scores]
            total = functools.reduce(jnp.add, weights)
            mixed = dot(jnp.concatenate([part.astype(BF) for part in weights], axis=1), values)
            m_ref[rows] = top
            l_ref[rows] = total if first else l_ref[rows] * factor + total
            acc_ref[rows] = mixed if first else acc_ref[rows] * factor + mixed

    late = z >= 5

    def attend_row(slot):
        hand[slot].wait_recv()

        @pl.when((z >= slot) & (~late if slot < 5 else late))
        def _():
            attend([kv[0, slot, k] for k in range(NY)], kv[1, slot].reshape(NY * TOK, 128))

        if slot < 5:

            @pl.when(late)
            def _():
                attend([kv[0, slot, k] for k in range(1, NY)], kv[1, slot, 1:].reshape((NY - 1) * TOK, 128))

    def attend_column():
        attend(
            [kv[0, slot, 0] for slot in range(1, 5)],
            jnp.concatenate([kv[1, slot, 0] for slot in range(1, 5)], axis=0),
        )

    attend([kv[0, 0, 0]], kv[1, 0, 0], first=True)
    pump(0, [0])
    hand_own[1].start()

    pair_b.wait_recv()
    pair_c.wait_recv()
    loads[6].wait()
    loads[9].wait()
    decay = jnp.exp(cum)
    inner = dot(crow[y, 0], brow[y, 0], NT) + dot(crow[y, 1], brow[y, 1], NT)
    for i in range(HEADS // 2):
        cols = slice(128 * i, 128 * (i + 1))
        x_two = x_ref[:, cols]
        parts = []
        for h in (2 * i, 2 * i + 1):
            gap = jnp.where(lower, cum[:, h : h + 1] - cum_t[h : h + 1, :], NEGATIVE)
            mix = (inner * jnp.exp(gap) * dt_t[h : h + 1, :]).astype(BF)
            parts.append(dot(mix, x_two))
        gain = jnp.where(left, skip_ref[:, 2 * i : 2 * i + 1], skip_ref[:, 2 * i + 1 : 2 * i + 2])
        gate = gate_ref[:, cols].astype(F32)
        gate = gate / (1.0 + jnp.exp(-gate))
        grow = jnp.where(left, decay[:, 2 * i : 2 * i + 1], decay[:, 2 * i + 1 : 2 * i + 2])
        yb[:, cols] = (jnp.where(left, parts[0], parts[1]) + gain * x_two.astype(F32)) * gate
        open_gate[:, cols] = gate * grow
        if i == 3:
            pump(1, [0])
            hand_own[2].start()
    pump(2, [0])
    hand_own[3].start()

    for k in range(1, NY):
        y_b[k].wait_recv()
        hand_b[k].start()
    loads[7].wait()
    for k in range(1, NY):
        y_pk[k].wait_recv()
        y_x[k].wait_recv()
    for k in range(1, NY):
        y_kv[k].start()
    for k in range(1, NY):
        y_c[k].start()
    for k in range(1, NY):
        hand_b[k].wait_recv()
    packed = prow[...]
    columns = packed.reshape(NY * 8, TOK).T

    def two_by_two(parts):
        return jnp.concatenate(
            [jnp.where(left, parts[0], parts[1]), jnp.where(left, parts[2], parts[3])], axis=1
        )

    logs = [two_by_two([packed[j, 4 + i : 5 + i] for i in range(4)]) for j in range(NY)]
    row_decay = jnp.exp(logs[0] + logs[1] + logs[2] + logs[3])
    state = None
    for j in range(NY):
        weight = two_by_two([columns[:, 8 * j + i : 8 * j + i + 1] for i in range(4)])
        weighted = (xrow[j].astype(F32) * weight).astype(BF)
        own = jnp.concatenate([dot(brow[j, 0], weighted, TN), dot(brow[j, 1], weighted, TN)], axis=0)
        state = own if state is None else state * jnp.exp(logs[j]) + own
        if j < NY - 1:
            prior[j + 1] = state.astype(BF)
    change[...] = state.reshape(PIECES, QW // PIECES, QW)
    pump(3, [0])
    hand_own[4].start()

    def share_row():
        for k in range(1, NY):
            y_kv[k].wait_recv()
            plus[0, NY - k].start()
        hand[0].start()

        for s in (5, 6, 7):

            @pl.when(z + s < NZ)
            def _():
                pl.semaphore_wait(ready.at[s - 5], 1)

            far[s].start()

    def row_part():
        for k in range(1, NY):
            y_c[k].wait_recv()
            hand_c[k].start()
        for k in range(1, NY):
            hand_c[k].wait_recv()
        for j in range(1, NY):
            early[j] = dot(crow[j, 0], prior[j, :128]) + dot(crow[j, 1], prior[j, 128:])

    def attend_own():
        hand[0].wait_recv()
        for k in range(1, NY):

            @pl.when(y + k >= NY)
            def _():
                attend([kv[0, 0, k]], kv[1, 0, k])


    @pl.when(z >= 4)
    def _():
        share_row()
        row_part()

    for copy in hand_own[1:]:
        copy.wait_recv()
    pl.when(late)(attend_column)
    pl.when(late)(attend_own)
    for i in range(PIECES):
        z_chain[i].wait_recv()
        rz[i] = (rin[i].astype(F32) * row_decay + change[i]).astype(BF)
        z_chain[i].start()

    @pl.when(z < 4)
    def _():
        share_row()
        row_part()

    entering = rin[...].reshape(QW, QW)
    before = jnp.zeros((1, QW), F32)
    for j in range(NY):
        part = dot(crow[j, 0], entering[:128]) + dot(crow[j, 1], entering[128:])
        if j > 0:
            before = before + logs[j - 1]
            part = part * jnp.exp(before) + early[j]
        gout[j] = part.astype(BF)
        y_out[j].start()
    fs[y] = gout[y]

    pump(0, [1, 2, 3])
    hand[1].start()
    pl.when(~late)(attend_own)
    pump(1, [1, 2, 3])
    hand[2].start()
    attend_row(1)
    for slot in (7, 6, 5):
        far[slot].wait_recv()
        hand[slot].start()
    attend_row(2)
    attend_row(7)
    attend_row(6)
    pump(2, [1, 2, 3])
    hand[3].start()
    attend_row(5)
    pump(3, [1, 2, 3])
    hand[4].start()
    attend_row(3)
    attend_row(4)
    for h in range(QH):
        rows = slice(h * TOK, (h + 1) * TOK)
        attn_out[:, h * 128 : (h + 1) * 128] = (acc_ref[rows] / jnp.sum(l_ref[rows], axis=1, keepdims=True)).astype(BF)

    for copy in y_in:
        copy.wait_recv()
    squares = jnp.zeros((TOK, 128), F32)
    for i in range(HEADS // 2):
        cols = slice(128 * i, 128 * (i + 1))
        part = fs[i // 2, :, 128 * (i % 2) : 128 * (i % 2) + 128].astype(F32)
        gated = yb[:, cols] + open_gate[:, cols] * part
        yb[:, cols] = gated
        squares = squares + gated * gated
    own_sum = jnp.sum(squares, axis=1, keepdims=True)
    sq_out[...] = jnp.broadcast_to(own_sum, (TOK, 128))
    swap.start()
    swap.wait_recv()
    mean = (sq_out[...] + sq_in[...]) * (1.0 / 2048)
    scale = lax.rsqrt(mean + EPSILON)
    for i in range(HEADS // 2):
        cols = slice(128 * i, 128 * (i + 1))
        ssm_out[:, cols] = (yb[:, cols] * scale * gain_ref[:, cols]).astype(BF)
    for copy in sends:
        copy.wait_send()


def hand_out(ssm, attention, ssm_out, attn_out):
    ssm_out[...] = ssm[...]
    attn_out[...] = attention[...]


def shards(
    ssm_input, ssm_gate, step_size, log_decay, input_b, input_c, skip_gain, norm_gain,
    attn_queries, attn_keys, attn_values,
):
    hbm = pl.BlockSpec(memory_space=pltpu.HBM)
    vmem = pl.BlockSpec(memory_space=pltpu.VMEM)
    dma = pltpu.SemaphoreType.DMA
    ssm, attention = pl.pallas_call(
        kernel,
        out_shape=(
            jax.ShapeDtypeStruct((TOK, 1024), BF),
            jax.ShapeDtypeStruct((TOK, 512), BF),
        ),
        in_specs=[hbm] * 6 + [vmem] * 2 + [hbm] * 3,
        out_specs=(vmem, vmem),
        scratch_shapes=[
            pltpu.VMEM((TOK, 1024), BF),
            pltpu.VMEM((TOK, 1024), BF),
            pltpu.VMEM((HEADS, TOK), F32),
            pltpu.VMEM((HEADS, TOK), F32),
            pltpu.VMEM((TOK, 512), BF),
            pltpu.VMEM((2, 64, TOK), BF),
            pltpu.VMEM((2, 64, TOK), BF),
            pltpu.VMEM((NY, 2, TOK, 128), BF),
            pltpu.VMEM((NY, 2, TOK, 128), BF),
            pltpu.VMEM((NY, TOK, QW), BF),
            pltpu.VMEM((NY, 8, TOK), F32),
            pltpu.VMEM((NY, 8, TOK), F32),
            pltpu.VMEM((PIECES, QW // PIECES, QW), F32),
            pltpu.VMEM((NY, QW, QW), BF),
            pltpu.VMEM((PIECES, QW // PIECES, QW), BF),
            pltpu.VMEM((PIECES, QW // PIECES, QW), BF),
            pltpu.VMEM((NY, TOK, QW), F32),
            pltpu.VMEM((NY, TOK, QW), BF),
            pltpu.VMEM((NY, TOK, QW), BF),
            pltpu.VMEM((2, NZ, NY, TOK, 128), BF),
            pltpu.VMEM((QH * TOK, 128), F32),
            pltpu.VMEM((QH * TOK, 128), F32),
            pltpu.VMEM((QH * TOK, 128), F32),
            pltpu.VMEM((QH * TOK, 128), BF),
            pltpu.VMEM((TOK, 1024), F32),
            pltpu.VMEM((TOK, 1024), F32),
            pltpu.VMEM((TOK, 128), F32),
            pltpu.VMEM((TOK, 128), F32),
            dma((10,)),
            dma((11,)),
            dma((11,)),
            dma((5, NY)),
            dma((5, NY)),
            dma((PIECES,)),
            dma((PIECES,)),
            dma((NY,)),
            dma((NY,)),
            dma((4, NY)),
            dma((4, NY)),
            dma((3,)),
            dma((3,)),
            dma((12,)),
            dma((12,)),
            pltpu.SemaphoreType.REGULAR((3,)),
        ],
        name="hybrid_mixer",
        compiler_params=pltpu.CompilerParams(
            collective_id=0, has_side_effects=True, vmem_limit_bytes=56 << 20
        ),
    )(
        ssm_input, ssm_gate, step_size.T, log_decay.T, input_b, input_c,
        skip_gain.reshape(1, HEADS), norm_gain.reshape(1, 1024),
        attn_queries, attn_keys.T, attn_values.T,
    )
    return pl.pallas_call(
        hand_out,
        out_shape=(
            jax.ShapeDtypeStruct((TOK, 1024), BF),
            jax.ShapeDtypeStruct((TOK, 512), BF),
        ),
        in_specs=[vmem] * 2,
        out_specs=(vmem, vmem),
        name="hand_out",
    )(ssm, attention)


def solution(mesh):
    split = P("ctx", "head")
    return jax.shard_map(
        shards,
        mesh=mesh,
        in_specs=(split,) * 6 + (P("head"), P("head")) + (split,) * 3,
        out_specs=(split, split),
        check_vma=False,
    )
```
